32 devices in a mesh: groups: 2 (over y), ep: 4 (over z), tp: 4 (over x, core).
Axes of the slice: x: 2, y: 2, z: 4, core: 2. Of those that a mesh axis runs over, the one named last changes fastest.
Arguments:
- resid: bfloat16 [256, 4096], P(('groups', 'ep'), 'tp'), parts along dimension 0, may hold values from -36 to 36
- query: bfloat16 [256, 4096], P(('groups', 'ep'), 'tp'), parts along dimension 0, may hold values from -4.5 to 4.5
- new_key: bfloat16 [256, 4096], P(('groups', 'ep'), 'tp'), parts along dimension 0, may hold values from -4.5 to 4.5
- new_value: bfloat16 [256, 4096], P(('groups', 'ep'), 'tp'), parts along dimension 0, may hold values from -4.5 to 4.5
- cache_keys: bfloat16 [256, 8, 4096], P(('groups', 'ep'), None, 'tp'), parts along dimension 0, may hold values from -4.5 to 4.5
- cache_values: bfloat16 [256, 8, 4096], P(('groups', 'ep'), None, 'tp'), parts along dimension 0, may hold values from -4.5 to 4.5
- cache_lengths: int32 [256], P(('groups', 'ep')), parts along dimension 0, may hold values from 2 to 8, as said below
- shallow_expert: int32 [256, 1], P(('groups', 'ep')), parts along dimension 0, may hold values from 0 to 3; in each aligned block of 32 rows (0 to 31, 32 to 63, ...) at most 12 rows name the same one
- shallow_gate: float32 [256], P(('groups', 'ep')), parts along dimension 0, may hold values from 0.2 to 1
- shallow_up: bfloat16 [4096, 32768], P('tp', 'ep'), may hold values from -0.09375 to 0.09375
- shallow_down: bfloat16 [32768, 4096], P('ep', 'tp'), may hold values from -0.0625 to 0.0625
- deep_expert: int32 [256, 1], P(('groups', 'ep')), parts along dimension 0, may hold values from 0 to 3; in each aligned block of 32 rows (0 to 31, 32 to 63, ...) at most 12 rows name the same one
- deep_gate: float32 [256], P(('groups', 'ep')), parts along dimension 0, may hold values from 0.2 to 1
- deep_up: bfloat16 [4096, 32768], P('tp', 'ep'), may hold values from -0.09375 to 0.09375
- deep_down: bfloat16 [32768, 4096], P('ep', 'tp'), may hold values from -0.0625 to 0.0625
Outputs:
- decoded: bfloat16 [256, 4096], P(('groups', 'ep'), 'tp'), parts along dimension 0
The draws below stay inside these ranges and needn't reach their ends.
There are 2 independent parts, one for each index of `groups`. The reference program is written for one: setup_inputs(seed, part) draws one part's arguments, and reference() takes and returns one part's arrays. A program takes and returns all parts, laid end to end along the dimension named above; an argument that names none is the same for every part. Nothing has to cross between parts.
Inputs may be any that keep to these rules, and one draw needn't show every extreme that they name: `cache_lengths`: some row holds exactly 8 positions. `shallow_expert`: of the rows of one ep index at most 12 name one expert, and exactly 12 do for some expert on some ep index. `deep_expert`: of the rows of one ep index at most 12 name one expert, and exactly 12 do for some expert on some ep index.
All inputs are finite; a program needn't handle non-finite values.
Results may differ from the reference program's by a relative error of at most 0.006.
Values may be sent and summed in bfloat16 or wider, within the bound.
No kernel may reach another device: no remote copies, remote signals or barrier semaphores. Data moves between devices by JAX's collectives and lax.ppermute only.
A program may use at most 192 MiB of HBM per device.

```python
import math
import jax
import jax.numpy as jnp
import numpy as np
from jax import lax

D = 4096
HEADS = 32
HD = 128
FF = 8192
EXPERTS = 4
ROWS_DEV = 32
CACHE = 8
ROWS = 128
CAP = 12
N_EP = 4


def draw_query(key, part):
    key = jax.random.fold_in(key, 11)
    values = jnp.clip(jax.random.normal(key, (ROWS, D), jnp.float32), -4.5, 4.5)
    return values.astype(jnp.bfloat16)


def draw_cache_keys(key, part):
    key = jax.random.fold_in(key, 12)
    values = jnp.clip(jax.random.normal(key, (ROWS, CACHE, D), jnp.float32), -4.5, 4.5)
    return values.astype(jnp.bfloat16)


def draw_resid(key, part):
    key = jax.random.fold_in(key, 13)
    base_key, column_key, row_key = jax.random.split(key, 3)
    rising = 0.5 + jnp.arange(D).astype(jnp.float32) / D
    column_scale = jnp.exp(jax.random.uniform(column_key, (D,), jnp.float32, math.log(0.3), math.log(3.0))) * rising
    row_scale = jnp.exp(jax.random.uniform(row_key, (ROWS, 1), jnp.float32, math.log(0.5), math.log(2.0)))
    base = jnp.clip(jax.random.normal(base_key, (ROWS, D), jnp.float32), -4.0, 4.0)
    values = base * column_scale[None, :] * row_scale
    return values.astype(jnp.bfloat16)


def draw_cache_lengths(key, part):
    key = jax.random.fold_in(key, 14)
    lengths = jax.random.randint(key, (ROWS,), 2, CACHE + 1)
    return lengths.at[0].set(CACHE).astype(jnp.int32)


def block_levels(rng, shape, shards, smallest, top_value):
    def one(axis_at, parts):
        steps = jax.random.uniform(jax.random.fold_in(jax.random.fold_in(rng, 6), axis_at), (parts,), jnp.float32, smallest / len(shards), top_value / len(shards))
        return jnp.repeat(jnp.exp(steps), shape[axis_at] // parts).reshape((-1,) + (1,) * (len(shape) - axis_at - 1))

    factor_of = one(*shards[0])
    for cut in shards[1:]:
        factor_of = factor_of * one(*cut)
    return factor_of


def routed_block(own_key, own, number, rows, amount, top, limit, lean):
    ranking = jax.random.permutation(own_key, amount)
    heavy_load, usual = portions_of(amount, rows * top, limit, lean, True), portions_of(amount, rows * top, limit, lean, False)
    places = jnp.arange(amount)

    def named(sizes, rotation):
        used = int((sizes > 0).sum())
        fixed = max(1, used // 4)
        moved = fixed + (places - fixed + rotation * (used - fixed)) % max(1, amount - fixed)
        return jnp.zeros((amount,), jnp.int32).at[ranking[jnp.where(places < fixed, places, moved)]].set(jnp.asarray(sizes, jnp.int32))

    sizes = jnp.where(number % 4 == 0, named(heavy_load, number // 4), named(usual, number - number // 4 - 1))
    mixed = jax.random.permutation(jax.random.fold_in(own, 3), amount)
    source_of, sink = mixed[0:amount // 2 * 2:2], mixed[1:amount // 2 * 2:2]
    room = jnp.minimum(sizes[source_of] - 1, limit - sizes[sink]) // 2
    room = jnp.where((source_of == ranking[0]) | (sink == ranking[0]) | (sizes[sink] == 0), 0, jnp.maximum(room, 0))
    moved = jax.random.randint(jax.random.fold_in(own, 4), (amount // 2,), 0, 1 << 20) % (room + 1)
    sizes = sizes.at[source_of].add(-moved).at[sink].add(moved)
    labels = jnp.searchsorted(jnp.cumsum(sizes), jnp.arange(rows * top), side="right").astype(jnp.int32)
    grid = labels.reshape(top, rows).T
    grid = grid[jax.random.permutation(jax.random.fold_in(own, 1), rows)]
    rotation = jax.random.randint(jax.random.fold_in(own, 2), (rows, 1), 0, top)
    return jnp.take_along_axis(grid, (jnp.arange(top)[None, :] + rotation) % top, axis=1)


def portions_of(number_of, total, bound, lean, full):
    portions = [(1 << 20) // math.isqrt(standing ** lean) + 1 for standing in range(1, number_of + 1)]
    largest = bound if full else min(bound, max(-(-total // number_of), total * portions[0] // sum(portions)))
    least = 1 if total - largest >= number_of - 1 else 0
    given, surplus = [largest] + [least] * (number_of - 1), total - largest - least * (number_of - 1)
    while surplus > 0:
        movable = [i for i in range(1, number_of) if given[i] < largest] or [i for i in range(1, number_of) if given[i] < bound]
        pool, budget = sum([portions[i] for i in movable]), surplus
        for i in movable:
            addition = min(bound - given[i], max(1, budget * portions[i] // pool), surplus)
            given[i] = given[i] + addition
            surplus = surplus - addition
    return np.array(given)


def scatter_about(key, shape, spread, limit, cuts=(), dtype=jnp.bfloat16):
    factor_of = block_levels(key, shape, cuts, -0.22, 0.18) if cuts else 1.0
    drawn = jax.random.normal(key, shape, jnp.float32) * spread * factor_of
    return jnp.minimum(jnp.maximum(drawn, -limit), limit).astype(dtype)


def setup_inputs(seed: int = 0, part: int = 0) -> dict:
    streams_of = jax.random.split(jax.random.key(seed), 16)
    part_splits = jax.random.split(jax.random.fold_in(streams_of[15], part), 16)
    resid = draw_resid(jax.random.fold_in(jax.random.fold_in(streams_of[15], part), 71), part)
    query = draw_query(jax.random.fold_in(jax.random.fold_in(streams_of[15], part), 71), part)
    new_key = scatter_about(part_splits[2], (ROWS, D), 1.0, 4.5, ((0, 4), (1, 4)))
    new_value = scatter_about(part_splits[3], (ROWS, D), 1.0, 4.5, ((0, 4), (1, 4)))
    cache_keys = draw_cache_keys(jax.random.fold_in(jax.random.fold_in(streams_of[15], part), 71), part)
    cache_values = scatter_about(part_splits[5], (ROWS, CACHE, D), 1.0, 4.5, ((0, 4), (2, 4)))
    cache_lengths = draw_cache_lengths(jax.random.fold_in(jax.random.fold_in(streams_of[15], part), 71), part)
    shallow_expert_keys = jax.random.split(jax.random.fold_in(part_splits[7], 1), ROWS // ROWS_DEV)
    shallow_expert_turns = jax.random.permutation(jax.random.fold_in(part_splits[7], 3), ROWS // ROWS_DEV)
    shallow_expert = jax.vmap(lambda own, number: routed_block(jax.random.fold_in(part_splits[7], 2), own, number, ROWS_DEV, EXPERTS, 1, CAP, 2))(shallow_expert_keys, shallow_expert_turns).reshape((ROWS, 1))
    shallow_gate = jnp.clip(0.2 + 0.8 * jax.random.uniform(part_splits[8], (ROWS,), jnp.float32) ** block_levels(part_splits[8], (ROWS,), ((0, 4),), -0.2, 0.2), 0.2, 1.0)
    shallow_up = scatter_about(streams_of[9], (D, EXPERTS * FF), D ** -0.5, 0.09375, ((0, 4), (1, 4)))
    shallow_down = scatter_about(streams_of[10], (EXPERTS * FF, D), FF ** -0.5, 0.0625, ((0, 4), (1, 4)))
    deep_expert_keys = jax.random.split(jax.random.fold_in(part_splits[11], 1), ROWS // ROWS_DEV)
    deep_expert_turns = jax.random.permutation(jax.random.fold_in(part_splits[11], 3), ROWS // ROWS_DEV)
    deep_expert = jax.vmap(lambda own, number: routed_block(jax.random.fold_in(part_splits[11], 2), own, number, ROWS_DEV, EXPERTS, 1, CAP, 1))(deep_expert_keys, deep_expert_turns).reshape((ROWS, 1))
    deep_gate = jnp.clip(0.2 + 0.8 * jax.random.uniform(part_splits[12], (ROWS,), jnp.float32) ** block_levels(part_splits[12], (ROWS,), ((0, 4),), -0.2, 0.2), 0.2, 1.0)
    deep_up = scatter_about(streams_of[13], (D, EXPERTS * FF), D ** -0.5, 0.09375, ((0, 4), (1, 4)))
    deep_down = scatter_about(streams_of[14], (EXPERTS * FF, D), FF ** -0.5, 0.0625, ((0, 4), (1, 4)))
    return dict(resid=resid, query=query, new_key=new_key, new_value=new_value, cache_keys=cache_keys, cache_values=cache_values, cache_lengths=cache_lengths, shallow_expert=shallow_expert, shallow_gate=shallow_gate, shallow_up=shallow_up, shallow_down=shallow_down, deep_expert=deep_expert, deep_gate=deep_gate, deep_up=deep_up, deep_down=deep_down)


epsilon = 1e-05

def attention(resid, query, new_key, new_value, cache_keys, cache_values, cache_lengths):
    queries = query.astype(jnp.float32).reshape(ROWS, HEADS, HD)
    own_keys = new_key.astype(jnp.float32).reshape(ROWS, HEADS, HD)
    own_values = new_value.astype(jnp.float32).reshape(ROWS, HEADS, HD)
    past_keys = cache_keys.astype(jnp.float32).reshape(ROWS, CACHE, HEADS, HD)
    past_values = cache_values.astype(jnp.float32).reshape(ROWS, CACHE, HEADS, HD)
    factor = 1.0 / math.sqrt(HD)
    cached = jnp.einsum('rhd,rjhd->rhj', queries, past_keys) * factor
    own_score = lax.optimization_barrier(jnp.sum(queries * own_keys, axis=-1)) * factor
    valid = jnp.arange(CACHE)[None, None, :] < cache_lengths[:, None, None]
    masked = jnp.where(valid, cached, -1e+30)
    highest = jnp.maximum(lax.optimization_barrier(jnp.max(masked, axis=-1)), own_score)
    cached_exp = jnp.where(valid, jnp.exp(masked - highest[..., None]), 0.0)
    own_exp = jnp.exp(own_score - highest)
    total = lax.optimization_barrier(jnp.sum(cached_exp, axis=-1)) + own_exp
    past_weights = lax.optimization_barrier((cached_exp / total[..., None]).astype(jnp.bfloat16)).astype(jnp.float32)
    own_weight = lax.optimization_barrier((own_exp / total).astype(jnp.bfloat16)).astype(jnp.float32)
    attended = jnp.einsum('rhj,rjhd->rhd', past_weights, past_values) + own_weight[..., None] * own_values
    return (resid.astype(jnp.float32) + attended.reshape(ROWS, D)).astype(jnp.bfloat16)

def expert_layer(states, expert_ids, gates, up_weight, down_weight):
    wide = states.astype(jnp.float32)
    center = lax.optimization_barrier(jnp.mean(wide, axis=1, keepdims=True))
    square = lax.optimization_barrier(jnp.mean(wide * wide, axis=1, keepdims=True))
    normalized = ((wide - center) * lax.rsqrt(square - center * center + epsilon)).astype(jnp.bfloat16)
    normalized = lax.optimization_barrier(normalized).astype(jnp.float32)
    padded = jnp.concatenate([normalized, jnp.zeros((1, D), jnp.float32)], axis=0)
    totals = jnp.zeros((ROWS + 1, D), jnp.float32)
    for expert in range(EXPERTS):
        member = expert_ids[:, 0] == expert
        picked = jnp.nonzero(member, size=N_EP * CAP, fill_value=ROWS)[0].astype(jnp.int32)
        chosen = padded[picked]
        up_cols = up_weight[:, expert * FF:(expert + 1) * FF].astype(jnp.float32)
        down_rows = down_weight[expert * FF:(expert + 1) * FF, :].astype(jnp.float32)
        pre = jnp.dot(chosen, up_cols, precision=lax.Precision.HIGHEST)
        hidden = lax.optimization_barrier(jax.nn.gelu(pre, approximate=True).astype(jnp.bfloat16)).astype(jnp.float32)
        produced = jnp.dot(hidden, down_rows, precision=lax.Precision.HIGHEST)
        totals = totals.at[picked].add(produced)
    return (wide + gates[:, None] * totals[:ROWS]).astype(jnp.bfloat16)

def reference(resid, query, new_key, new_value, cache_keys, cache_values, cache_lengths, shallow_expert, shallow_gate, shallow_up, shallow_down, deep_expert, deep_gate, deep_up, deep_down):
    shallow_in = attention(resid, query, new_key, new_value, cache_keys, cache_values, cache_lengths)
    shallow_out = expert_layer(shallow_in, shallow_expert, shallow_gate, shallow_up, shallow_down)
    return expert_layer(shallow_out, deep_expert, deep_gate, deep_up, deep_down)
```

```python
import functools
import math

import jax
import jax.numpy as jnp
from jax import lax
from jax.experimental import pallas as pl
from jax.experimental.pallas import tpu as pltpu
from jax.sharding import PartitionSpec as P

D = 4096
HD = 128
EXPERTS = 4
CAP = 12


epsilon = 1e-05


def attention(resid, query, new_key, new_value, cache_keys, cache_values, cache_lengths):
    row_count, feature_count = resid.shape
    heads_here = feature_count // HD
    depth = cache_keys.shape[1]
    queries = query.reshape(row_count, heads_here, HD)
    own_keys = new_key.reshape(row_count, heads_here, HD)
    own_values = new_value.reshape(row_count, heads_here, HD)
    past_keys = cache_keys.reshape(row_count, depth, heads_here, HD)
    past_values = cache_values.reshape(row_count, depth, heads_here, HD)
    factor = 1.0 / math.sqrt(HD)
    cached = (
        jnp.einsum("rhd,rjhd->rhj", queries, past_keys, preferred_element_type=jnp.float32) * factor
    )
    own_score = (
        jnp.einsum("rhd,rhd->rh", queries, own_keys, preferred_element_type=jnp.float32) * factor
    )
    valid = jnp.arange(depth)[None, None, :] < cache_lengths[:, None, None]
    masked = jnp.where(valid, cached, -1e30)
    highest = jnp.maximum(jnp.max(masked, axis=-1), own_score)
    cached_exp = jnp.where(valid, jnp.exp(masked - highest[..., None]), 0.0)
    own_exp = jnp.exp(own_score - highest)
    total = jnp.sum(cached_exp, axis=-1) + own_exp
    past_weights = (cached_exp / total[..., None]).astype(jnp.bfloat16)
    own_weight = (own_exp / total).astype(jnp.bfloat16)
    attended = jnp.einsum(
        "rhj,rjhd->rhd", past_weights, past_values, preferred_element_type=jnp.float32
    )
    attended = attended + own_weight.astype(jnp.float32)[..., None] * own_values.astype(jnp.float32)
    return (resid.astype(jnp.float32) + attended.reshape(row_count, feature_count)).astype(
        jnp.bfloat16
    )


def expert_layer(states, expert_ids, gates, up_weight, down_weight):
    row_count, feature_count = states.shape
    ep_count = lax.axis_size("ep")
    sharing = ep_count // EXPERTS
    mine = lax.axis_index("ep") // sharing
    wide = states.astype(jnp.float32)
    row_sum, row_square = lax.psum((jnp.sum(wide, axis=1), jnp.sum(wide * wide, axis=1)), "tp")
    center = row_sum / D
    spread = row_square / D - center * center
    normalized = ((wide - center[:, None]) * lax.rsqrt(spread + epsilon)[:, None]).astype(
        jnp.bfloat16
    )
    slots = CAP
    routed = expert_ids[:, 0]
    onehot = (routed[:, None] == jnp.arange(EXPERTS)[None, :]).astype(jnp.int32)
    earlier = jnp.cumsum(onehot, axis=0) - onehot
    rank_in = jnp.sum(earlier * onehot, axis=1)
    position = routed * slots + rank_in
    placing = (position[None, :] == jnp.arange(EXPERTS * slots)[:, None]).astype(jnp.bfloat16)
    compact = jnp.dot(placing, normalized, preferred_element_type=jnp.float32).astype(jnp.bfloat16)
    compact = compact.reshape(EXPERTS, slots, feature_count)
    chosen = lax.dynamic_index_in_dim(
        lax.all_gather(compact[None], "ep", axis=0, tiled=True), mine, axis=1, keepdims=False
    )
    pre = jnp.einsum("scd,df->scf", chosen, up_weight, preferred_element_type=jnp.float32)
    hidden_width = pre.shape[2]
    flat_pre = pre.reshape(ep_count * slots, hidden_width)
    summed = lax.psum(flat_pre, "tp")
    activated = jax.nn.gelu(summed, approximate=True).astype(jnp.bfloat16)
    partial_value = jnp.dot(activated, down_weight, preferred_element_type=jnp.float32)
    returned = lax.all_to_all(
        partial_value.reshape(ep_count, slots, feature_count),
        "ep",
        split_axis=0,
        concat_axis=0,
        tiled=True,
    )
    combined = jnp.sum(returned.reshape(EXPERTS, sharing, slots, feature_count), axis=1)
    combined = combined.reshape(EXPERTS * slots, feature_count)
    produced = jnp.take(combined, position, axis=0)
    return (wide + gates[:, None] * produced).astype(jnp.bfloat16)


def general_body(
    resid,
    query,
    new_key,
    new_value,
    cache_keys,
    cache_values,
    cache_lengths,
    shallow_expert,
    shallow_gate,
    shallow_up,
    shallow_down,
    deep_expert,
    deep_gate,
    deep_up,
    deep_down,
):
    shallow_in = attention(
        resid, query, new_key, new_value, cache_keys, cache_values, cache_lengths
    )
    shallow_out = expert_layer(shallow_in, shallow_expert, shallow_gate, shallow_up, shallow_down)
    return expert_layer(shallow_out, deep_expert, deep_gate, deep_up, deep_down)


SLOTS = EXPERTS * CAP
PAD = 16
TALL = 56
META = 128
MIB = 1 << 20
F32 = jnp.float32
BF16 = jnp.bfloat16


def iota(shape, dim):
    return lax.broadcasted_iota(jnp.int32, shape, dim)


def to_column(row, count):
    same = iota((count, count), 0) == iota((count, count), 1)
    return jnp.sum(jnp.where(same, row, jnp.zeros_like(row)), axis=1, keepdims=True)


def to_row(column, count):
    same = iota((count, count), 0) == iota((count, count), 1)
    return jnp.sum(jnp.where(same, column, jnp.zeros_like(column)), axis=0, keepdims=True)


def ranks(id_row, id_column, count):
    earlier = iota((count, count), 1) < iota((count, count), 0)
    same = (id_row == id_column) & earlier
    return jnp.sum(same.astype(jnp.int32), axis=1, keepdims=True)


def split3(value):
    high = value.astype(BF16).astype(F32)
    middle = (value - high).astype(BF16).astype(F32)
    low = (value - high - middle).astype(BF16).astype(F32)
    return high, middle, low


def dot(left, right):
    return jnp.dot(left, right, preferred_element_type=F32)


def params(mib):
    return pltpu.CompilerParams(vmem_limit_bytes=mib * MIB)


def cost(flops, moved):
    return pl.CostEstimate(flops=flops, bytes_accessed=moved, transcendentals=0)


VM = pl.BlockSpec(memory_space=pltpu.VMEM)
SM = pl.BlockSpec(memory_space=pltpu.SMEM)


def attend_kernel(
    place_ref, resid_ref, query_ref, key_ref, value_ref, keys_ref, values_ref, length_ref,
    shallow_ref, sgate_ref, deep_ref, dgate_ref, out0, out1, out2, out3,
):
    rows, features = resid_ref.shape
    depth = keys_ref.shape[1]
    flat = rows * depth
    factor = 1.0 / math.sqrt(HD)
    spread = (iota((features, META), 0) // HD == iota((features, META), 1)).astype(BF16)
    gather = (iota((META, features), 1) // HD == iota((META, features), 0)).astype(BF16)

    def head_sums(products):
        high = products.astype(BF16)
        low = (products - high.astype(F32)).astype(BF16)
        return dot(high, spread) + dot(low, spread)

    query = query_ref[...].astype(F32)
    own = head_sums(query * key_ref[...].astype(F32)) * factor
    products = query[:, None, :] * keys_ref[...].astype(F32)
    cached = head_sums(products.reshape(flat, features)) * factor
    repeated = iota((flat, rows), 0) // depth == iota((flat, rows), 1)
    length = jnp.sum(jnp.where(repeated, length_ref[...], 0), axis=1, keepdims=True)
    valid = (iota((flat, META), 0) % depth) < length
    masked = jnp.where(valid, cached, -1e30).reshape(rows, depth, META)
    highest = jnp.maximum(jnp.max(masked, axis=1), own)
    past = jnp.exp(masked - highest[:, None, :])
    past = jnp.where(valid, past.reshape(flat, META), 0.0).reshape(rows, depth, META)
    own_exp = jnp.exp(own - highest)
    total = jnp.sum(past, axis=1) + own_exp
    weights = (past / total[:, None, :]).reshape(flat, META).astype(BF16)
    own_weight = (own_exp / total).astype(BF16)
    wide = dot(weights, gather).reshape(rows, depth, features)
    attended = jnp.sum(wide * values_ref[...].astype(F32), axis=1)
    attended = attended + dot(own_weight, gather) * value_ref[...].astype(F32)
    states = (resid_ref[...].astype(F32) + attended).astype(BF16)

    here = place_ref[1]
    shallow = shallow_ref[...]
    deep = deep_ref[...]
    shallow_column = to_column(shallow, rows)
    deep_column = to_column(deep, rows)
    place = (shallow_column ^ here) * PAD + ranks(shallow, shallow_column, rows)
    lane = iota((rows, META), 1)
    notes = jnp.where(lane == 0, deep_column.astype(F32), 0.0)
    notes = jnp.where(lane == 1, ranks(deep, deep_column, rows).astype(F32), notes)
    for start, gate_ref in ((2, sgate_ref), (5, dgate_ref)):
        for at, piece in enumerate(split3(to_column(gate_ref[...], rows))):
            notes = jnp.where(lane == start + at, piece, notes)
    notes = jnp.where(lane == 8, 1.0, notes)
    full = jnp.concatenate([states, notes.astype(BF16)], axis=1)
    choose = (iota((EXPERTS * PAD, rows), 0) == to_row(place, rows)).astype(BF16)
    sent = dot(choose, full)
    for at, out in enumerate((out0, out1, out2, out3)):
        out[...] = sent[at * PAD : (at + 1) * PAD].astype(BF16)


def attend(place, arrays):
    rows, features = arrays[0].shape
    shape = jax.ShapeDtypeStruct((PAD, features + META), BF16)
    return pl.pallas_call(
        attend_kernel,
        in_specs=[SM] + [VM] * len(arrays),
        out_specs=[VM] * 4,
        out_shape=[shape] * 4,
        compiler_params=params(24),
        name="attend",
    )(place, *arrays)


def choose_shallow():
    source = iota((TALL, EXPERTS * PAD), 1)
    kept = jnp.where(source % PAD < CAP, source // PAD * CAP + source % PAD, -1)
    return (kept == iota((TALL, EXPERTS * PAD), 0)).astype(BF16)


def choose_deep(here, held, features):
    notes = held[:, features:].astype(F32)
    count = held.shape[0]
    number = iota((count, 1), 0)
    apart = (number // SLOTS) ^ (number % SLOTS // CAP)
    place = apart * CAP + notes[:, 1:2].astype(jnp.int32)
    mine = (notes[:, 0:1].astype(jnp.int32) == here) & (notes[:, 8:9] > 0.5)
    place = jnp.where(mine, place, -1)
    return (iota((TALL, count), 0) == to_row(place, count)).astype(BF16)


def up_block(rows, means, weights):
    product = dot(rows, weights)
    columns = product[SLOTS : SLOTS + 1]
    row = iota(product.shape, 0)
    centred = product - means * columns
    return row, centred, columns


def up_first_kernel(deep, place_ref, h0, h1, h2, h3, weight_ref, sent_ref, rows_ref, stats_ref):
    features = weight_ref.shape[0]

    @pl.when(pl.program_id(0) == 0)
    def _():
        held = jnp.concatenate([h0[...], h1[...], h2[...], h3[...]], axis=0)
        choose = choose_deep(place_ref[1], held, features) if deep else choose_shallow()
        picked = dot(choose, held)
        ones = (iota(picked.shape, 0) == SLOTS) & (iota(picked.shape, 1) < features)
        rows_ref[...] = jnp.where(ones, 1.0, picked).astype(BF16)
        wide = picked[:, :features]
        lane = iota((TALL, META), 1)
        total = jnp.sum(wide, axis=1, keepdims=True)
        square = jnp.sum(wide * wide, axis=1, keepdims=True)
        stats_ref[...] = jnp.where(lane == 0, total, jnp.where(lane == 1, square, 0.0))

    means = stats_ref[:, 0:1] / features
    row, centred, columns = up_block(rows_ref[:, :features], means, weight_ref[...])
    high = columns.astype(BF16).astype(F32)
    tail = jnp.where(row == SLOTS, high, jnp.where(row == SLOTS + 1, columns - high, 0.0))
    sent_ref[...] = jnp.where(row < SLOTS, centred, tail).astype(BF16)


def up_first(deep, place, held, weights, step):
    features, width = weights.shape
    half = width // 2
    count = half // step
    return pl.pallas_call(
        functools.partial(up_first_kernel, deep),
        grid_spec=pltpu.PrefetchScalarGridSpec(
            num_scalar_prefetch=1,
            grid=(count,),
            in_specs=[pl.BlockSpec(h.shape, lambda i, p: (0, 0)) for h in held]
            + [pl.BlockSpec((features, step), lambda i, p: (0, (1 - p[0]) * count + i))],
            out_specs=[
                pl.BlockSpec((TALL, step), lambda i, p: (0, i)),
                pl.BlockSpec((TALL, features + META), lambda i, p: (0, 0)),
                pl.BlockSpec((TALL, META), lambda i, p: (0, 0)),
            ],
        ),
        out_shape=[
            jax.ShapeDtypeStruct((TALL, half), BF16),
            jax.ShapeDtypeStruct((TALL, features + META), BF16),
            jax.ShapeDtypeStruct((TALL, META), F32),
        ],
        compiler_params=params(40),
        cost_estimate=cost(2 * TALL * features * half, 2 * features * half),
        name="up_first",
    )(place, *held, weights)


def up_second_kernel(place_ref, rows_ref, stats_ref, weight_ref, kept_ref):
    features = weight_ref.shape[0]
    means = stats_ref[:, 0:1] / features
    row, centred, columns = up_block(rows_ref[:, :features], means, weight_ref[...])
    kept_ref[...] = jnp.where(row < SLOTS, centred, jnp.where(row == SLOTS, columns, 0.0))


def up_second(place, rows, stats, weights, step):
    features, width = weights.shape
    half = width // 2
    count = half // step
    return pl.pallas_call(
        up_second_kernel,
        grid_spec=pltpu.PrefetchScalarGridSpec(
            num_scalar_prefetch=1,
            grid=(count,),
            in_specs=[
                pl.BlockSpec(rows.shape, lambda i, p: (0, 0)),
                pl.BlockSpec(stats.shape, lambda i, p: (0, 0)),
                pl.BlockSpec((features, step), lambda i, p: (0, p[0] * count + i)),
            ],
            out_specs=pl.BlockSpec((TALL, step), lambda i, p: (0, i)),
        ),
        out_shape=jax.ShapeDtypeStruct((TALL, half), F32),
        compiler_params=params(40),
        cost_estimate=cost(2 * TALL * features * half, 2 * features * half),
        name="up_second",
    )(place, rows, stats, weights)


def merge_kernel(features, kept_ref, got_ref, stats_ref, got_stats_ref, sent_ref, sum_ref, sums_ref):
    width = kept_ref.shape[1]
    stats, other = stats_ref[...], got_stats_ref[...]
    apart = (stats[:, 0:1] - other[:, 0:1]) * (0.5 / features)
    sums = stats + other
    sums_ref[...] = sums
    step = 512
    for at in range(0, width, step):
        kept = kept_ref[:, at : at + step]
        got = got_ref[:, at : at + step].astype(F32)
        mine = kept[SLOTS : SLOTS + 1]
        theirs = got[SLOTS : SLOTS + 1] + got[SLOTS + 1 : SLOTS + 2]
        row = iota(kept.shape, 0)
        columns = mine + theirs
        merged = jnp.where(row < SLOTS, kept + got + apart * (mine - theirs), columns)
        sum_ref[:, at : at + step] = merged
        high = columns.astype(BF16).astype(F32)
        tail = jnp.where(row == SLOTS, high, jnp.where(row == SLOTS + 1, columns - high, 0.0))
        sent_ref[:, at : at + step] = jnp.where(row < SLOTS, merged, tail).astype(BF16)
    lane = iota((TALL, META), 1)
    packed = jnp.zeros((TALL, META), F32)
    for which in range(2):
        for at, piece in enumerate(split3(sums[:, which : which + 1])):
            packed = jnp.where(lane == 3 * which + at, piece, packed)
    sent_ref[:, width:] = packed.astype(BF16)


def merge(features, kept, got, stats, got_stats):
    width = kept.shape[1]
    return pl.pallas_call(
        functools.partial(merge_kernel, features),
        in_specs=[VM] * 4,
        out_specs=[VM] * 3,
        out_shape=[
            jax.ShapeDtypeStruct((TALL, width + META), BF16),
            jax.ShapeDtypeStruct((TALL, width), F32),
            jax.ShapeDtypeStruct((TALL, META), F32),
        ],
        compiler_params=params(16),
        name="merge",
    )(kept, got, stats, got_stats)


def hidden_kernel(features, sum_ref, sums_ref, got_ref, hidden_ref):
    width = sum_ref.shape[1]
    packed = got_ref[:, width:].astype(F32)
    theirs_total = packed[:, 0:1] + packed[:, 1:2] + packed[:, 2:3]
    theirs_square = packed[:, 3:4] + packed[:, 4:5] + packed[:, 5:6]
    total, square = sums_ref[:, 0:1], sums_ref[:, 1:2]
    apart = (total - theirs_total) * (0.5 / (2 * features))
    center = (total + theirs_total) / D
    spread = (square + theirs_square) / D - center * center
    scale = lax.rsqrt(spread + epsilon)
    step = 512
    for at in range(0, width, step):
        mine = sum_ref[:, at : at + step]
        got = got_ref[:, at : at + step].astype(F32)
        columns = mine[SLOTS : SLOTS + 1] - (got[SLOTS : SLOTS + 1] + got[SLOTS + 1 : SLOTS + 2])
        pre = ((mine + got + apart * columns) * scale)[:SLOTS]
        hidden_ref[:, at : at + step] = jax.nn.gelu(pre, approximate=True).astype(BF16)


def hidden_units(features, total, sums, got):
    return pl.pallas_call(
        functools.partial(hidden_kernel, features),
        in_specs=[VM] * 3,
        out_specs=VM,
        out_shape=jax.ShapeDtypeStruct((SLOTS, total.shape[1]), BF16),
        compiler_params=params(16),
        name="hidden",
    )(total, sums, got)


def down_first_kernel(place_ref, hidden_ref, weight_ref, out_ref):
    @pl.when(pl.program_id(0) == 0)
    def _():
        out_ref[...] = jnp.zeros_like(out_ref)

    out_ref[...] += dot(hidden_ref[...], weight_ref[...])


def down_first(place, hidden, weights, step):
    width, features = weights.shape
    half = width // 2
    count = half // step
    return pl.pallas_call(
        down_first_kernel,
        grid_spec=pltpu.PrefetchScalarGridSpec(
            num_scalar_prefetch=1,
            grid=(count,),
            in_specs=[
                pl.BlockSpec((SLOTS, step), lambda i, p: (0, i)),
                pl.BlockSpec((step, features), lambda i, p: (p[0] * count + i, 0)),
            ],
            out_specs=pl.BlockSpec((SLOTS, features), lambda i, p: (0, 0)),
        ),
        out_shape=jax.ShapeDtypeStruct((SLOTS, features), F32),
        compiler_params=params(40),
        cost_estimate=cost(2 * SLOTS * features * half, 2 * features * half),
        name="down_first",
    )(place, hidden, weights)


def down_second_kernel(deep, place_ref, part_ref, rows_ref, hidden_ref, weight_ref, *rest):
    outs, total_ref = rest[:-1], rest[-1]
    features = weight_ref.shape[1]

    @pl.when(pl.program_id(0) == 0)
    def _():
        total_ref[...] = part_ref[...]

    total_ref[...] += dot(hidden_ref[...], weight_ref[...])

    @pl.when(pl.program_id(0) == pl.num_programs(0) - 1)
    def _():
        rows = rows_ref[...].astype(F32)[:SLOTS]
        notes = rows[:, features:]
        first = 5 if deep else 2
        gate = notes[:, first : first + 1] + notes[:, first + 1 : first + 2]
        gate = gate + notes[:, first + 2 : first + 3]
        result = rows[:, :features] + gate * total_ref[...]
        if not deep:
            outs[0][...] = jnp.concatenate([result, notes], axis=1).astype(BF16)
        else:
            target = iota((EXPERTS * PAD, SLOTS), 0)
            kept = jnp.where(target % PAD < CAP, target // PAD * CAP + target % PAD, -1)
            spread = (kept == iota((EXPERTS * PAD, SLOTS), 1)).astype(BF16)
            placed = dot(spread, result.astype(BF16))
            for at, out in enumerate(outs):
                out[...] = placed[at * PAD : (at + 1) * PAD].astype(BF16)


def down_second(deep, place, part, rows, hidden, weights, step):
    width, features = weights.shape
    half = width // 2
    count = half // step
    fixed = lambda i, p: (0, 0)
    shapes = [(PAD, features)] * EXPERTS if deep else [(SLOTS, features + META)]
    return pl.pallas_call(
        functools.partial(down_second_kernel, deep),
        grid_spec=pltpu.PrefetchScalarGridSpec(
            num_scalar_prefetch=1,
            grid=(count,),
            in_specs=[
                pl.BlockSpec(part.shape, fixed),
                pl.BlockSpec(rows.shape, fixed),
                pl.BlockSpec((SLOTS, step), lambda i, p: (0, i)),
                pl.BlockSpec((step, features), lambda i, p: ((1 - p[0]) * count + i, 0)),
            ],
            out_specs=[pl.BlockSpec(shape, fixed) for shape in shapes],
            scratch_shapes=[pltpu.VMEM((SLOTS, features), F32)],
        ),
        out_shape=[jax.ShapeDtypeStruct(shape, BF16) for shape in shapes],
        compiler_params=params(40),
        cost_estimate=cost(2 * SLOTS * features * half, 2 * features * half),
        name="down_second",
    )(place, part, rows, hidden, weights)


def finish_kernel(place_ref, deep_ref, g0, g1, g2, g3, out_ref):
    rows = out_ref.shape[0]
    deep = deep_ref[...]
    column = to_column(deep, rows)
    place = (column ^ place_ref[1]) * PAD + ranks(deep, column, rows)
    choose = (iota((rows, EXPERTS * PAD), 1) == place).astype(BF16)
    held = jnp.concatenate([g0[...], g1[...], g2[...], g3[...]], axis=0)
    out_ref[...] = dot(choose, held).astype(BF16)


def finish(place, deep, got, rows):
    return pl.pallas_call(
        finish_kernel,
        in_specs=[SM] + [VM] * 5,
        out_specs=VM,
        out_shape=jax.ShapeDtypeStruct((rows, got[0].shape[1]), BF16),
        compiler_params=params(16),
        name="finish",
    )(place, deep, *got)


def swap(value, axis, apart):
    count = lax.axis_size(axis)
    return lax.ppermute(value, axis, [(i, i ^ apart) for i in range(count)])


def swap_all(blocks):
    return [blocks[0]] + [swap(blocks[k], "ep", k) for k in (1, 2, 3)]


def expert_block(deep, place, held, up, down):
    features = up.shape[0]
    step = min(1024, up.shape[1] // 2)
    sent, rows, stats = up_first(deep, place, held, up, step)
    got, got_stats = swap(sent, "tp", 1), swap(stats, "tp", 1)
    kept = up_second(place, rows, stats, up, step)
    sent, total, sums = merge(features, kept, got, stats, got_stats)
    hidden = hidden_units(features, total, sums, swap(sent, "tp", 2))
    other = swap(hidden, "tp", 1)
    part = down_first(place, hidden, down, step)
    return down_second(deep, place, part, rows, other, down, step)


def fast_body(
    resid,
    query,
    new_key,
    new_value,
    cache_keys,
    cache_values,
    cache_lengths,
    shallow_expert,
    shallow_gate,
    shallow_up,
    shallow_down,
    deep_expert,
    deep_gate,
    deep_up,
    deep_down,
):
    rows = resid.shape[0]
    place = jnp.stack([lax.axis_index("tp") % 2, lax.axis_index("ep")]).astype(jnp.int32)
    deep_ids = deep_expert.reshape(1, rows)
    blocks = attend(
        place,
        (
            resid,
            query,
            new_key,
            new_value,
            cache_keys,
            cache_values,
            cache_lengths.reshape(1, rows),
            shallow_expert.reshape(1, rows),
            shallow_gate.reshape(1, rows),
            deep_ids,
            deep_gate.reshape(1, rows),
        ),
    )
    held = swap_all(blocks)
    (after,) = expert_block(False, place, held, shallow_up, shallow_down)
    held = swap_all([after] * EXPERTS)
    blocks = expert_block(True, place, held, deep_up, deep_down)
    return finish(place, deep_ids, swap_all(blocks), rows)


def solution(mesh):
    fits = mesh.shape["ep"] == EXPERTS and mesh.shape["tp"] == 4
    return jax.shard_map(
        fast_body if fits else general_body,
        mesh=mesh,
        in_specs=(
            P(("groups", "ep"), "tp"),
            P(("groups", "ep"), "tp"),
            P(("groups", "ep"), "tp"),
            P(("groups", "ep"), "tp"),
            P(("groups", "ep"), None, "tp"),
            P(("groups", "ep"), None, "tp"),
            P(("groups", "ep")),
            P(("groups", "ep"), None),
            P(("groups", "ep")),
            P("tp", "ep"),
            P("ep", "tp"),
            P(("groups", "ep"), None),
            P(("groups", "ep")),
            P("tp", "ep"),
            P("ep", "tp"),
        ),
        out_specs=P(("groups", "ep"), "tp"),
        check_vma=False,
    )
```

```python
import functools
import math

import jax
import jax.numpy as jnp
from jax import lax
from jax.experimental import pallas as pl
from jax.experimental.pallas import tpu as pltpu
from jax.sharding import PartitionSpec as P

D = 4096
HD = 128
EXPERTS = 4
CAP = 12


epsilon = 1e-05


def attention(resid, query, new_key, new_value, cache_keys, cache_values, cache_lengths):
    row_count, feature_count = resid.shape
    heads_here = feature_count // HD
    depth = cache_keys.shape[1]
    queries = query.reshape(row_count, heads_here, HD)
    own_keys = new_key.reshape(row_count, heads_here, HD)
    own_values = new_value.reshape(row_count, heads_here, HD)
    past_keys = cache_keys.reshape(row_count, depth, heads_here, HD)
    past_values = cache_values.reshape(row_count, depth, heads_here, HD)
    factor = 1.0 / math.sqrt(HD)
    cached = (
        jnp.einsum("rhd,rjhd->rhj", queries, past_keys, preferred_element_type=jnp.float32) * factor
    )
    own_score = (
        jnp.einsum("rhd,rhd->rh", queries, own_keys, preferred_element_type=jnp.float32) * factor
    )
    valid = jnp.arange(depth)[None, None, :] < cache_lengths[:, None, None]
    masked = jnp.where(valid, cached, -1e30)
    highest = jnp.maximum(jnp.max(masked, axis=-1), own_score)
    cached_exp = jnp.where(valid, jnp.exp(masked - highest[..., None]), 0.0)
    own_exp = jnp.exp(own_score - highest)
    total = jnp.sum(cached_exp, axis=-1) + own_exp
    past_weights = (cached_exp / total[..., None]).astype(jnp.bfloat16)
    own_weight = (own_exp / total).astype(jnp.bfloat16)
    attended = jnp.einsum(
        "rhj,rjhd->rhd", past_weights, past_values, preferred_element_type=jnp.float32
    )
    attended = attended + own_weight.astype(jnp.float32)[..., None] * own_values.astype(jnp.float32)
    return (resid.astype(jnp.float32) + attended.reshape(row_count, feature_count)).astype(
        jnp.bfloat16
    )


def expert_layer(states, expert_ids, gates, up_weight, down_weight):
    row_count, feature_count = states.shape
    ep_count = lax.axis_size("ep")
    sharing = ep_count // EXPERTS
    mine = lax.axis_index("ep") // sharing
    wide = states.astype(jnp.float32)
    row_sum, row_square = lax.psum((jnp.sum(wide, axis=1), jnp.sum(wide * wide, axis=1)), "tp")
    center = row_sum / D
    spread = row_square / D - center * center
    normalized = ((wide - center[:, None]) * lax.rsqrt(spread + epsilon)[:, None]).astype(
        jnp.bfloat16
    )
    slots = CAP
    routed = expert_ids[:, 0]
    onehot = (routed[:, None] == jnp.arange(EXPERTS)[None, :]).astype(jnp.int32)
    earlier = jnp.cumsum(onehot, axis=0) - onehot
    rank_in = jnp.sum(earlier * onehot, axis=1)
    position = routed * slots + rank_in
    placing = (position[None, :] == jnp.arange(EXPERTS * slots)[:, None]).astype(jnp.bfloat16)
    compact = jnp.dot(placing, normalized, preferred_element_type=jnp.float32).astype(jnp.bfloat16)
    compact = compact.reshape(EXPERTS, slots, feature_count)
    chosen = lax.dynamic_index_in_dim(
        lax.all_gather(compact[None], "ep", axis=0, tiled=True), mine, axis=1, keepdims=False
    )
    pre = jnp.einsum("scd,df->scf", chosen, up_weight, preferred_element_type=jnp.float32)
    hidden_width = pre.shape[2]
    flat_pre = pre.reshape(ep_count * slots, hidden_width)
    summed = lax.psum(flat_pre, "tp")
    activated = jax.nn.gelu(summed, approximate=True).astype(jnp.bfloat16)
    partial_value = jnp.dot(activated, down_weight, preferred_element_type=jnp.float32)
    returned = lax.all_to_all(
        partial_value.reshape(ep_count, slots, feature_count),
        "ep",
        split_axis=0,
        concat_axis=0,
        tiled=True,
    )
    combined = jnp.sum(returned.reshape(EXPERTS, sharing, slots, feature_count), axis=1)
    combined = combined.reshape(EXPERTS * slots, feature_count)
    produced = jnp.take(combined, position, axis=0)
    return (wide + gates[:, None] * produced).astype(jnp.bfloat16)


def general_body(
    resid,
    query,
    new_key,
    new_value,
    cache_keys,
    cache_values,
    cache_lengths,
    shallow_expert,
    shallow_gate,
    shallow_up,
    shallow_down,
    deep_expert,
    deep_gate,
    deep_up,
    deep_down,
):
    shallow_in = attention(
        resid, query, new_key, new_value, cache_keys, cache_values, cache_lengths
    )
    shallow_out = expert_layer(shallow_in, shallow_expert, shallow_gate, shallow_up, shallow_down)
    return expert_layer(shallow_out, deep_expert, deep_gate, deep_up, deep_down)


SLOTS = EXPERTS * CAP
PAD = 16
TALL = 56
META = 128
MIB = 1 << 20
STEP = 1024
FIRST_SHARE = 0.5
F32 = jnp.float32
BF16 = jnp.bfloat16


def iota(shape, dim):
    return lax.broadcasted_iota(jnp.int32, shape, dim)


def to_column(row, count):
    same = iota((count, count), 0) == iota((count, count), 1)
    return jnp.sum(jnp.where(same, row, jnp.zeros_like(row)), axis=1, keepdims=True)


def to_row(column, count):
    same = iota((count, count), 0) == iota((count, count), 1)
    return jnp.sum(jnp.where(same, column, jnp.zeros_like(column)), axis=0, keepdims=True)


def ranks(id_row, id_column, count):
    earlier = iota((count, count), 1) < iota((count, count), 0)
    same = (id_row == id_column) & earlier
    return jnp.sum(same.astype(jnp.int32), axis=1, keepdims=True)


def split3(value):
    high = value.astype(BF16).astype(F32)
    middle = (value - high).astype(BF16).astype(F32)
    low = (value - high - middle).astype(BF16).astype(F32)
    return high, middle, low


def dot(left, right):
    return jnp.dot(left, right, preferred_element_type=F32)


def params(mib):
    return pltpu.CompilerParams(vmem_limit_bytes=mib * MIB)


def cost(flops, moved):
    return pl.CostEstimate(flops=flops, bytes_accessed=moved, transcendentals=0)


VM = pl.BlockSpec(memory_space=pltpu.VMEM)
SM = pl.BlockSpec(memory_space=pltpu.SMEM)
HB = pl.BlockSpec(memory_space=pltpu.HBM)


def attend_kernel(
    place_ref, resid_in, query_in, key_in, value_in, keys_in, values_in, length_in,
    shallow_in, sgate_in, deep_in, dgate_in, out0, out1, out2, out3, home_ref,
    resid_ref, query_ref, key_ref, value_ref, keys_ref, values_ref, length_ref,
    shallow_ref, sgate_ref, deep_ref, dgate_ref, sems,
):
    rows, features = resid_ref.shape
    depth = keys_ref.shape[1]
    flat = rows * depth
    factor = 1.0 / math.sqrt(HD)
    order = (
        (query_in, query_ref), (keys_in, keys_ref), (key_in, key_ref), (length_in, length_ref),
        (values_in, values_ref), (value_in, value_ref), (resid_in, resid_ref),
        (shallow_in, shallow_ref), (sgate_in, sgate_ref), (deep_in, deep_ref), (dgate_in, dgate_ref),
    )
    copies = [pltpu.make_async_copy(a, b, sems.at[i]) for i, (a, b) in enumerate(order)]
    for copy in copies:
        copy.start()
    spread = (iota((features, META), 0) // HD == iota((features, META), 1)).astype(BF16)
    gather = (iota((META, features), 1) // HD == iota((META, features), 0)).astype(BF16)

    def head_sums(products):
        high = products.astype(BF16)
        low = (products - high.astype(F32)).astype(BF16)
        return dot(high, spread) + dot(low, spread)

    for copy in copies[:4]:
        copy.wait()
    query = query_ref[...].astype(F32)
    own = head_sums(query * key_ref[...].astype(F32)) * factor
    products = query[:, None, :] * keys_ref[...].astype(F32)
    cached = head_sums(products.reshape(flat, features)) * factor
    repeated = iota((flat, rows), 0) // depth == iota((flat, rows), 1)
    length = jnp.sum(jnp.where(repeated, length_ref[...], 0), axis=1, keepdims=True)
    valid = (iota((flat, META), 0) % depth) < length
    masked = jnp.where(valid, cached, -1e30).reshape(rows, depth, META)
    highest = jnp.maximum(jnp.max(masked, axis=1), own)
    past = jnp.exp(masked - highest[:, None, :])
    past = jnp.where(valid, past.reshape(flat, META), 0.0).reshape(rows, depth, META)
    own_exp = jnp.exp(own - highest)
    total = jnp.sum(past, axis=1) + own_exp
    weights = (past / total[:, None, :]).reshape(flat, META).astype(BF16)
    own_weight = (own_exp / total).astype(BF16)
    for copy in copies[4:]:
        copy.wait()
    wide = dot(weights, gather).reshape(rows, depth, features)
    attended = jnp.sum(wide * values_ref[...].astype(F32), axis=1)
    attended = attended + dot(own_weight, gather) * value_ref[...].astype(F32)
    states = (resid_ref[...].astype(F32) + attended).astype(BF16)

    here = place_ref[1]
    shallow = shallow_ref[...]
    deep = deep_ref[...]
    shallow_column = to_column(shallow, rows)
    deep_column = to_column(deep, rows)
    place = (shallow_column ^ here) * PAD + ranks(shallow, shallow_column, rows)
    lane = iota((rows, META), 1)
    notes = jnp.where(lane == 0, deep_column.astype(F32), 0.0)
    deep_rank = ranks(deep, deep_column, rows)
    home_ref[...] = jnp.broadcast_to((deep_column ^ here) * PAD + deep_rank, (rows, META))
    notes = jnp.where(lane == 1, deep_rank.astype(F32), notes)
    for start, gate_ref in ((2, sgate_ref), (5, dgate_ref)):
        for at, piece in enumerate(split3(to_column(gate_ref[...], rows))):
            notes = jnp.where(lane == start + at, piece, notes)
    notes = jnp.where(lane == 8, 1.0, notes)
    full = jnp.concatenate([states, notes.astype(BF16)], axis=1)
    choose = (iota((EXPERTS * PAD, rows), 0) == to_row(place, rows)).astype(BF16)
    sent = dot(choose, full)
    for at, out in enumerate((out0, out1, out2, out3)):
        out[...] = sent[at * PAD : (at + 1) * PAD].astype(BF16)


def attend(place, arrays):
    rows, features = arrays[0].shape
    shape = jax.ShapeDtypeStruct((PAD, features + META), BF16)
    return pl.pallas_call(
        attend_kernel,
        in_specs=[SM] + [HB] * len(arrays),
        out_specs=[VM] * 5,
        out_shape=[shape] * 4 + [jax.ShapeDtypeStruct((rows, META), jnp.int32)],
        scratch_shapes=[pltpu.VMEM(a.shape, a.dtype) for a in arrays]
        + [pltpu.SemaphoreType.DMA((len(arrays),))],
        compiler_params=params(16),
        name="attend",
    )(place, *[pltpu.with_memory_space_constraint(a, pltpu.HBM) for a in arrays])


def load_kernel(weight_ref, after_ref, out_ref, sems):
    count = sems.shape[0]
    rows = weight_ref.shape[0] // count
    copies = [
        pltpu.make_async_copy(
            weight_ref.at[pl.ds(i * rows, rows)], out_ref.at[pl.ds(i * rows, rows)], sems.at[i]
        )
        for i in range(count)
    ]
    for copy in copies:
        copy.start()
    for copy in copies:
        copy.wait()


def load(weights, after):
    return pl.pallas_call(
        load_kernel,
        in_specs=[HB, pl.BlockSpec(memory_space=pl.ANY)],
        out_specs=VM,
        out_shape=jax.ShapeDtypeStruct(weights.shape, weights.dtype),
        scratch_shapes=[pltpu.SemaphoreType.DMA((4,))],
        compiler_params=params(4),
        cost_estimate=cost(0, 2 * weights.size),
        name="load",
    )(pltpu.with_memory_space_constraint(weights, pltpu.HBM), after)


def choose_shallow():
    source = iota((TALL, EXPERTS * PAD), 1)
    kept = jnp.where(source % PAD < CAP, source // PAD * CAP + source % PAD, -1)
    return (kept == iota((TALL, EXPERTS * PAD), 0)).astype(BF16)


def choose_deep(here, held, features):
    notes = held[:, features:].astype(F32)
    count = held.shape[0]
    number = iota((count, 1), 0)
    apart = (number // SLOTS) ^ (number % SLOTS // CAP)
    place = apart * CAP + notes[:, 1:2].astype(jnp.int32)
    mine = (notes[:, 0:1].astype(jnp.int32) == here) & (notes[:, 8:9] > 0.5)
    place = jnp.where(mine, place, -1)
    return (iota((TALL, count), 0) == to_row(place, count)).astype(BF16)


def up_block(rows, means, weights):
    product = dot(rows, weights)
    columns = product[SLOTS : SLOTS + 1]
    row = iota(product.shape, 0)
    centred = product - means * columns
    return row, centred, columns


def cuts_of(half):
    unit = 4 * META
    first = max(unit, int(half * FIRST_SHARE) // unit * unit)
    return (0, first), (first, half - first)


def columns_at(place_ref, weight_ref, own, at, step):
    half = weight_ref.shape[1] // 2
    which = place_ref[0] if own else 1 - place_ref[0]
    return weight_ref[:, pl.ds(pl.multiple_of(which * half + at, 128), step)]


def steps_of(width):
    return [(at, min(STEP, width - at)) for at in range(0, width, STEP)]


def up_first_kernel(deep, cuts, place_ref, h0, h1, h2, h3, weight_ref, rows_ref, stats_ref, *sent):
    features = weight_ref.shape[0]
    held = jnp.concatenate([h0[...], h1[...], h2[...], h3[...]], axis=0)
    choose = choose_deep(place_ref[1], held, features) if deep else choose_shallow()
    picked = dot(choose, held)
    ones = (iota(picked.shape, 0) == SLOTS) & (iota(picked.shape, 1) < features)
    rows_ref[...] = jnp.where(ones, 1.0, picked).astype(BF16)
    wide = picked[:, :features]
    lane = iota((TALL, META), 1)
    total = jnp.sum(wide, axis=1, keepdims=True)
    square = jnp.sum(wide * wide, axis=1, keepdims=True)
    stats_ref[...] = jnp.where(lane == 0, total, jnp.where(lane == 1, square, 0.0))
    means = total / features
    for (start, width), sent_ref in zip(cuts, sent):
        for at, step in steps_of(width):
            weights = columns_at(place_ref, weight_ref, False, start + at, step)
            row, centred, columns = up_block(rows_ref[:, :features], means, weights)
            high = columns.astype(BF16).astype(F32)
            tail = jnp.where(row == SLOTS, high, jnp.where(row == SLOTS + 1, columns - high, 0.0))
            sent_ref[:, at : at + step] = jnp.where(row < SLOTS, centred, tail).astype(BF16)


def up_first(deep, cuts, place, held, weights):
    features, width = weights.shape
    half = width // 2
    return pl.pallas_call(
        functools.partial(up_first_kernel, deep, cuts),
        in_specs=[SM] + [VM] * 5,
        out_specs=[VM] * 4,
        out_shape=[
            jax.ShapeDtypeStruct((TALL, features + META), BF16),
            jax.ShapeDtypeStruct((TALL, META), F32),
        ]
        + [jax.ShapeDtypeStruct((TALL, cut[1]), BF16) for cut in cuts],
        compiler_params=params(8),
        cost_estimate=cost(2 * TALL * features * half, 2 * features * half),
        name="up_first",
    )(place, *held, weights)


def up_second_kernel(start, place_ref, rows_ref, stats_ref, weight_ref, kept_ref):
    features = weight_ref.shape[0]
    means = stats_ref[:, 0:1] / features
    for at, step in steps_of(kept_ref.shape[1]):
        weights = columns_at(place_ref, weight_ref, True, start + at, step)
        row, centred, columns = up_block(rows_ref[:, :features], means, weights)
        kept_ref[:, at : at + step] = jnp.where(
            row < SLOTS, centred, jnp.where(row == SLOTS, columns, 0.0)
        )


def up_second(place, rows, stats, weights, cut):
    start, width = cut
    features = weights.shape[0]
    return pl.pallas_call(
        functools.partial(up_second_kernel, start),
        in_specs=[SM] + [VM] * 3,
        out_specs=VM,
        out_shape=jax.ShapeDtypeStruct((TALL, width), F32),
        compiler_params=params(8),
        cost_estimate=cost(2 * TALL * features * width, 2 * features * width),
        name="up_second",
    )(place, rows, stats, weights)


def merge_into(features, source, width, got_ref, stats, other, sum_ref, sent_ref):
    apart = (stats[:, 0:1] - other[:, 0:1]) * (0.5 / features)
    held = jnp.zeros((SLOTS, META), F32)
    slot = iota((SLOTS, META), 0)
    for at, step in steps_of(width):
        kept = source(at, step)
        got = got_ref[:, at : at + step].astype(F32)
        mine = kept[SLOTS : SLOTS + 1]
        theirs = got[SLOTS : SLOTS + 1] + got[SLOTS + 1 : SLOTS + 2]
        row = iota(kept.shape, 0)
        columns = mine + theirs
        merged = jnp.where(row < SLOTS, kept + got + apart * (mine - theirs), columns)
        sum_ref[:, at : at + step] = merged
        sent_ref[:, at : at + step] = merged[:SLOTS].astype(BF16)
        for part in range(0, step, META):
            held = jnp.where(slot == (at + part) // META, columns[:, part : part + META], held)
    sent_ref[:, width : width + META] = held.astype(BF16)


def merge_kernel(features, kept_ref, got_ref, stats_ref, got_stats_ref, sent_ref, sum_ref, sums_ref):
    width = kept_ref.shape[1]
    stats, other = stats_ref[...], got_stats_ref[...]
    sums = stats + other
    sums_ref[...] = sums
    source = lambda at, step: kept_ref[:, at : at + step]
    merge_into(features, source, width, got_ref, stats, other, sum_ref, sent_ref)
    lane = iota((SLOTS, META), 1)
    packed = jnp.zeros((SLOTS, META), F32)
    for which in range(2):
        for at, piece in enumerate(split3(sums[:SLOTS, which : which + 1])):
            packed = jnp.where(lane == 3 * which + at, piece, packed)
    sent_ref[:, width + META :] = packed.astype(BF16)


def merge(features, kept, got, stats, got_stats):
    width = kept.shape[1]
    return pl.pallas_call(
        functools.partial(merge_kernel, features),
        in_specs=[VM] * 4,
        out_specs=[VM] * 3,
        out_shape=[
            jax.ShapeDtypeStruct((SLOTS, width + 2 * META), BF16),
            jax.ShapeDtypeStruct((TALL, width), F32),
            jax.ShapeDtypeStruct((TALL, META), F32),
        ],
        compiler_params=params(8),
        name="merge",
    )(kept, got, stats, got_stats)


def up_merge_kernel(
    start, place_ref, rows_ref, stats_ref, got_stats_ref, weight_ref, got_ref, sent_ref, sum_ref
):
    features = weight_ref.shape[0]
    stats = stats_ref[...]
    means = stats[:, 0:1] / features

    def source(at, step):
        weights = columns_at(place_ref, weight_ref, True, start + at, step)
        row, centred, columns = up_block(rows_ref[:, :features], means, weights)
        return jnp.where(row < SLOTS, centred, jnp.where(row == SLOTS, columns, 0.0))

    merge_into(features, source, sum_ref.shape[1], got_ref, stats, got_stats_ref[...], sum_ref, sent_ref)


def up_merge(place, rows, stats, got_stats, weights, got, cut):
    start, width = cut
    features = weights.shape[0]
    return pl.pallas_call(
        functools.partial(up_merge_kernel, start),
        in_specs=[SM] + [VM] * 5,
        out_specs=[VM] * 2,
        out_shape=[
            jax.ShapeDtypeStruct((SLOTS, width + META), BF16),
            jax.ShapeDtypeStruct((TALL, width), F32),
        ],
        compiler_params=params(8),
        cost_estimate=cost(2 * TALL * features * width, 2 * features * width),
        name="up_merge",
    )(place, rows, stats, got_stats, weights, got)


def hidden_kernel(features, sum_ref, sums_ref, got_ref, packed_ref, hidden_ref):
    width = sum_ref.shape[1]
    packed = packed_ref[:, packed_ref.shape[1] - META :].astype(F32)
    held = got_ref[:, width : width + META].astype(F32)
    theirs_total = packed[:, 0:1] + packed[:, 1:2] + packed[:, 2:3]
    theirs_square = packed[:, 3:4] + packed[:, 4:5] + packed[:, 5:6]
    total, square = sums_ref[:SLOTS, 0:1], sums_ref[:SLOTS, 1:2]
    apart = (total - theirs_total) * (0.5 / (2 * features))
    center = (total + theirs_total) / D
    spread = (square + theirs_square) / D - center * center
    scale = lax.rsqrt(spread + epsilon)
    step = 4 * META
    for at in range(0, width, step):
        mine = sum_ref[:, at : at + step]
        got = got_ref[:, at : at + step].astype(F32)
        first = at // META
        theirs = jnp.concatenate([held[i : i + 1] for i in range(first, first + step // META)], axis=1)
        columns = mine[SLOTS : SLOTS + 1] - theirs
        pre = (mine[:SLOTS] + got + apart * columns) * scale
        hidden_ref[:, at : at + step] = jax.nn.gelu(pre, approximate=True).astype(BF16)


def hidden_units(features, total, sums, got, packed):
    return pl.pallas_call(
        functools.partial(hidden_kernel, features),
        in_specs=[VM] * 4,
        out_specs=VM,
        out_shape=jax.ShapeDtypeStruct((SLOTS, total.shape[1]), BF16),
        compiler_params=params(8),
        cost_estimate=cost(1, 1),
        name="hidden",
    )(total, sums, got, packed)


def rows_at(place_ref, weight_ref, own, start, width):
    half = weight_ref.shape[0] // 2
    which = place_ref[0] if own else 1 - place_ref[0]
    return weight_ref[pl.ds(pl.multiple_of(which * half + start, 128), width), :]


def down_part_kernel(own, start, place_ref, hidden_ref, weight_ref, *rest):
    *earlier, out_ref = rest
    product = dot(hidden_ref[...], rows_at(place_ref, weight_ref, own, start, hidden_ref.shape[1]))
    for part in earlier:
        product = product + part[...]
    out_ref[...] = product


def down_part(place, hidden, weights, own, cut, *earlier):
    start, width = cut
    features = weights.shape[1]
    return pl.pallas_call(
        functools.partial(down_part_kernel, own, start),
        in_specs=[SM] + [VM] * (2 + len(earlier)),
        out_specs=VM,
        out_shape=jax.ShapeDtypeStruct((SLOTS, features), F32),
        compiler_params=params(8),
        cost_estimate=cost(1, 1),
        name="down_part",
    )(place, hidden, weights, *earlier)


def down_last_kernel(deep, start, place_ref, part_ref, rows_ref, hidden_ref, weight_ref, *outs):
    features = weight_ref.shape[1]
    weights = rows_at(place_ref, weight_ref, False, start, hidden_ref.shape[1])
    total = part_ref[...] + dot(hidden_ref[...], weights)
    rows = rows_ref[...].astype(F32)[:SLOTS]
    notes = rows[:, features:]
    first = 5 if deep else 2
    gate = notes[:, first : first + 1] + notes[:, first + 1 : first + 2]
    gate = gate + notes[:, first + 2 : first + 3]
    result = rows[:, :features] + gate * total
    if not deep:
        outs[0][...] = jnp.concatenate([result, notes], axis=1).astype(BF16)
    else:
        target = iota((EXPERTS * PAD, SLOTS), 0)
        kept = jnp.where(target % PAD < CAP, target // PAD * CAP + target % PAD, -1)
        spread = (kept == iota((EXPERTS * PAD, SLOTS), 1)).astype(BF16)
        placed = dot(spread, result.astype(BF16))
        for at, out in enumerate(outs):
            out[...] = placed[at * PAD : (at + 1) * PAD].astype(BF16)


def down_last(deep, place, part, rows, hidden, weights, cut):
    start, width = cut
    features = weights.shape[1]
    shapes = [(PAD, features)] * EXPERTS if deep else [(SLOTS, features + META)]
    return pl.pallas_call(
        functools.partial(down_last_kernel, deep, start),
        in_specs=[SM] + [VM] * 4,
        out_specs=[VM] * len(shapes),
        out_shape=[jax.ShapeDtypeStruct(shape, BF16) for shape in shapes],
        compiler_params=params(8),
        cost_estimate=cost(2 * SLOTS * features * width, 2 * features * width),
        name="down_last",
    )(place, part, rows, hidden, weights)


def finish_kernel(home_ref, g0, g1, g2, g3, out_ref):
    rows = out_ref.shape[0]
    choose = (iota((rows, EXPERTS * PAD), 1) == home_ref[:, 0:1]).astype(BF16)
    held = jnp.concatenate([g0[...], g1[...], g2[...], g3[...]], axis=0)
    out_ref[...] = dot(choose, held).astype(BF16)


def finish(home, got):
    return pl.pallas_call(
        finish_kernel,
        in_specs=[VM] * 5,
        out_specs=VM,
        out_shape=jax.ShapeDtypeStruct((home.shape[0], got[0].shape[1]), BF16),
        compiler_params=params(8),
        name="finish",
    )(home, *got)


def swap(value, axis, apart):
    count = lax.axis_size(axis)
    return lax.ppermute(value, axis, [(i, i ^ apart) for i in range(count)])


def swap_all(blocks):
    return [blocks[0]] + [swap(blocks[k], "ep", k) for k in (1, 2, 3)]


def after(value, earlier):
    return lax.optimization_barrier((value, earlier))[0]


def expert_block(deep, place, held, up, down):
    features, width = up.shape
    first, second = cuts = cuts_of(width // 2)
    rows, stats, sent_a, sent_b = up_first(deep, cuts, place, held, up)
    got_a, got_stats = swap(sent_a, "tp", 1), swap(stats, "tp", 1)
    got_b = swap(sent_b, "tp", 1)
    kept = up_second(place, rows, stats, up, first)
    sent_a, total_a, sums = merge(features, kept, got_a, stats, got_stats)
    over_a = swap(sent_a, "tp", 2)
    later = after(rows, sent_a)
    sent_b, total_b = up_merge(place, later, stats, got_stats, up, got_b, second)
    over_b = swap(sent_b, "tp", 2)
    hidden_a = hidden_units(features, after(total_a, sent_b), sums, over_a, over_a)
    other_a = swap(hidden_a, "tp", 1)
    part = down_part(place, hidden_a, down, True, first)
    part = down_part(place, other_a, down, False, first, part)
    hidden_b = hidden_units(features, after(total_b, part), sums, over_b, over_a)
    other_b = swap(hidden_b, "tp", 1)
    part = down_part(place, hidden_b, down, True, second, part)
    return down_last(deep, place, part, rows, other_b, down, second)


def fast_body(
    resid,
    query,
    new_key,
    new_value,
    cache_keys,
    cache_values,
    cache_lengths,
    shallow_expert,
    shallow_gate,
    shallow_up,
    shallow_down,
    deep_expert,
    deep_gate,
    deep_up,
    deep_down,
):
    rows = resid.shape[0]
    place = jnp.stack([lax.axis_index("tp") % 2, lax.axis_index("ep")]).astype(jnp.int32)
    *blocks, home = attend(
        place,
        (
            resid,
            query,
            new_key,
            new_value,
            cache_keys,
            cache_values,
            cache_lengths.reshape(1, rows),
            shallow_expert.reshape(1, rows),
            shallow_gate.reshape(1, rows),
            deep_expert.reshape(1, rows),
            deep_gate.reshape(1, rows),
        ),
    )
    weights = load(shallow_up, blocks[0])
    (between,) = expert_block(False, place, swap_all(blocks), weights, shallow_down)
    blocks = expert_block(True, place, swap_all([between] * EXPERTS), deep_up, deep_down)
    return finish(home, swap_all(blocks))


def solution(mesh):
    fits = mesh.shape["ep"] == EXPERTS and mesh.shape["tp"] == 4
    return jax.shard_map(
        fast_body if fits else general_body,
        mesh=mesh,
        in_specs=(
            P(("groups", "ep"), "tp"),
            P(("groups", "ep"), "tp"),
            P(("groups", "ep"), "tp"),
            P(("groups", "ep"), "tp"),
            P(("groups", "ep"), None, "tp"),
            P(("groups", "ep"), None, "tp"),
            P(("groups", "ep")),
            P(("groups", "ep"), None),
            P(("groups", "ep")),
            P("tp", "ep"),
            P("ep", "tp"),
            P(("groups", "ep"), None),
            P(("groups", "ep")),
            P("tp", "ep"),
            P("ep", "tp"),
        ),
        out_specs=P(("groups", "ep"), "tp"),
        check_vma=False,
    )
```

```python
import functools
import math

import jax
import jax.numpy as jnp
from jax import lax
from jax.experimental import pallas as pl
from jax.experimental.pallas import tpu as pltpu
from jax.sharding import PartitionSpec as P

D = 4096
HD = 128
EXPERTS = 4
CAP = 12


epsilon = 1e-05


def attention(resid, query, new_key, new_value, cache_keys, cache_values, cache_lengths):
    row_count, feature_count = resid.shape
    heads_here = feature_count // HD
    depth = cache_keys.shape[1]
    queries = query.reshape(row_count, heads_here, HD)
    own_keys = new_key.reshape(row_count, heads_here, HD)
    own_values = new_value.reshape(row_count, heads_here, HD)
    past_keys = cache_keys.reshape(row_count, depth, heads_here, HD)
    past_values = cache_values.reshape(row_count, depth, heads_here, HD)
    factor = 1.0 / math.sqrt(HD)
    cached = (
        jnp.einsum("rhd,rjhd->rhj", queries, past_keys, preferred_element_type=jnp.float32) * factor
    )
    own_score = (
        jnp.einsum("rhd,rhd->rh", queries, own_keys, preferred_element_type=jnp.float32) * factor
    )
    valid = jnp.arange(depth)[None, None, :] < cache_lengths[:, None, None]
    masked = jnp.where(valid, cached, -1e30)
    highest = jnp.maximum(jnp.max(masked, axis=-1), own_score)
    cached_exp = jnp.where(valid, jnp.exp(masked - highest[..., None]), 0.0)
    own_exp = jnp.exp(own_score - highest)
    total = jnp.sum(cached_exp, axis=-1) + own_exp
    past_weights = (cached_exp / total[..., None]).astype(jnp.bfloat16)
    own_weight = (own_exp / total).astype(jnp.bfloat16)
    attended = jnp.einsum(
        "rhj,rjhd->rhd", past_weights, past_values, preferred_element_type=jnp.float32
    )
    attended = attended + own_weight.astype(jnp.float32)[..., None] * own_values.astype(jnp.float32)
    return (resid.astype(jnp.float32) + attended.reshape(row_count, feature_count)).astype(
        jnp.bfloat16
    )


def expert_layer(states, expert_ids, gates, up_weight, down_weight):
    row_count, feature_count = states.shape
    ep_count = lax.axis_size("ep")
    sharing = ep_count // EXPERTS
    mine = lax.axis_index("ep") // sharing
    wide = states.astype(jnp.float32)
    row_sum, row_square = lax.psum((jnp.sum(wide, axis=1), jnp.sum(wide * wide, axis=1)), "tp")
    center = row_sum / D
    spread = row_square / D - center * center
    normalized = ((wide - center[:, None]) * lax.rsqrt(spread + epsilon)[:, None]).astype(
        jnp.bfloat16
    )
    slots = CAP
    routed = expert_ids[:, 0]
    onehot = (routed[:, None] == jnp.arange(EXPERTS)[None, :]).astype(jnp.int32)
    earlier = jnp.cumsum(onehot, axis=0) - onehot
    rank_in = jnp.sum(earlier * onehot, axis=1)
    position = routed * slots + rank_in
    placing = (position[None, :] == jnp.arange(EXPERTS * slots)[:, None]).astype(jnp.bfloat16)
    compact = jnp.dot(placing, normalized, preferred_element_type=jnp.float32).astype(jnp.bfloat16)
    compact = compact.reshape(EXPERTS, slots, feature_count)
    chosen = lax.dynamic_index_in_dim(
        lax.all_gather(compact[None], "ep", axis=0, tiled=True), mine, axis=1, keepdims=False
    )
    pre = jnp.einsum("scd,df->scf", chosen, up_weight, preferred_element_type=jnp.float32)
    hidden_width = pre.shape[2]
    flat_pre = pre.reshape(ep_count * slots, hidden_width)
    summed = lax.psum(flat_pre, "tp")
    activated = jax.nn.gelu(summed, approximate=True).astype(jnp.bfloat16)
    partial_value = jnp.dot(activated, down_weight, preferred_element_type=jnp.float32)
    returned = lax.all_to_all(
        partial_value.reshape(ep_count, slots, feature_count),
        "ep",
        split_axis=0,
        concat_axis=0,
        tiled=True,
    )
    combined = jnp.sum(returned.reshape(EXPERTS, sharing, slots, feature_count), axis=1)
    combined = combined.reshape(EXPERTS * slots, feature_count)
    produced = jnp.take(combined, position, axis=0)
    return (wide + gates[:, None] * produced).astype(jnp.bfloat16)


def general_body(
    resid,
    query,
    new_key,
    new_value,
    cache_keys,
    cache_values,
    cache_lengths,
    shallow_expert,
    shallow_gate,
    shallow_up,
    shallow_down,
    deep_expert,
    deep_gate,
    deep_up,
    deep_down,
):
    shallow_in = attention(
        resid, query, new_key, new_value, cache_keys, cache_values, cache_lengths
    )
    shallow_out = expert_layer(shallow_in, shallow_expert, shallow_gate, shallow_up, shallow_down)
    return expert_layer(shallow_out, deep_expert, deep_gate, deep_up, deep_down)


SLOTS = EXPERTS * CAP
PAD = 16
TALL = 56
META = 128
MIB = 1 << 20
STEP = 1024
FIRST_SHARE = 0.5
F32 = jnp.float32
BF16 = jnp.bfloat16


def iota(shape, dim):
    return lax.broadcasted_iota(jnp.int32, shape, dim)


def to_column(row, count):
    same = iota((count, count), 0) == iota((count, count), 1)
    return jnp.sum(jnp.where(same, row, jnp.zeros_like(row)), axis=1, keepdims=True)


def to_row(column, count):
    same = iota((count, count), 0) == iota((count, count), 1)
    return jnp.sum(jnp.where(same, column, jnp.zeros_like(column)), axis=0, keepdims=True)


def ranks(id_row, id_column, count):
    earlier = iota((count, count), 1) < iota((count, count), 0)
    same = (id_row == id_column) & earlier
    return jnp.sum(same.astype(jnp.int32), axis=1, keepdims=True)


def split3(value):
    high = value.astype(BF16).astype(F32)
    middle = (value - high).astype(BF16).astype(F32)
    low = (value - high - middle).astype(BF16).astype(F32)
    return high, middle, low


def core_here():
    return lax.axis_index("tp") & 1


def dot(left, right):
    return jnp.dot(left, right, preferred_element_type=F32)


def params(mib):
    return pltpu.CompilerParams(vmem_limit_bytes=mib * MIB)


def cost(flops, moved):
    return pl.CostEstimate(flops=flops, bytes_accessed=moved, transcendentals=0)


VM = pl.BlockSpec(memory_space=pltpu.VMEM)
HB = pl.BlockSpec(memory_space=pltpu.HBM)


def attend_kernel(
    resid_in, query_in, key_in, value_in, keys_in, values_in, length_in,
    shallow_in, sgate_in, deep_in, dgate_in, out0, out1, out2, out3, home_ref,
    resid_ref, query_ref, key_ref, value_ref, keys_ref, values_ref, length_ref,
    shallow_ref, sgate_ref, deep_ref, dgate_ref, sems,
):
    rows, features = resid_ref.shape
    depth = keys_ref.shape[1]
    flat = rows * depth
    factor = 1.0 / math.sqrt(HD)
    order = (
        (query_in, query_ref), (keys_in, keys_ref), (key_in, key_ref), (length_in, length_ref),
        (values_in, values_ref), (value_in, value_ref), (resid_in, resid_ref),
        (shallow_in, shallow_ref), (sgate_in, sgate_ref), (deep_in, deep_ref), (dgate_in, dgate_ref),
    )
    copies = [pltpu.make_async_copy(a, b, sems.at[i]) for i, (a, b) in enumerate(order)]
    for copy in copies:
        copy.start()
    spread = (iota((features, META), 0) // HD == iota((features, META), 1)).astype(BF16)
    gather = (iota((META, features), 1) // HD == iota((META, features), 0)).astype(BF16)

    def head_sums(products):
        high = products.astype(BF16)
        low = (products - high.astype(F32)).astype(BF16)
        return dot(high, spread) + dot(low, spread)

    for copy in copies[:4]:
        copy.wait()
    query = query_ref[...].astype(F32)
    own = head_sums(query * key_ref[...].astype(F32)) * factor
    products = query[:, None, :] * keys_ref[...].astype(F32)
    cached = head_sums(products.reshape(flat, features)) * factor
    repeated = iota((flat, rows), 0) // depth == iota((flat, rows), 1)
    length = jnp.sum(jnp.where(repeated, length_ref[...], 0), axis=1, keepdims=True)
    valid = (iota((flat, META), 0) % depth) < length
    masked = jnp.where(valid, cached, -1e30).reshape(rows, depth, META)
    highest = jnp.maximum(jnp.max(masked, axis=1), own)
    past = jnp.exp(masked - highest[:, None, :])
    past = jnp.where(valid, past.reshape(flat, META), 0.0).reshape(rows, depth, META)
    own_exp = jnp.exp(own - highest)
    total = jnp.sum(past, axis=1) + own_exp
    weights = (past / total[:, None, :]).reshape(flat, META).astype(BF16)
    own_weight = (own_exp / total).astype(BF16)
    for copy in copies[4:]:
        copy.wait()
    wide = dot(weights, gather).reshape(rows, depth, features)
    attended = jnp.sum(wide * values_ref[...].astype(F32), axis=1)
    attended = attended + dot(own_weight, gather) * value_ref[...].astype(F32)
    states = (resid_ref[...].astype(F32) + attended).astype(BF16)

    here = lax.axis_index("ep")
    shallow = shallow_ref[...]
    deep = deep_ref[...]
    shallow_column = to_column(shallow, rows)
    deep_column = to_column(deep, rows)
    place = (shallow_column ^ here) * PAD + ranks(shallow, shallow_column, rows)
    lane = iota((rows, META), 1)
    notes = jnp.where(lane == 0, deep_column.astype(F32), 0.0)
    deep_rank = ranks(deep, deep_column, rows)
    home_ref[...] = jnp.broadcast_to((deep_column ^ here) * PAD + deep_rank, (rows, META))
    notes = jnp.where(lane == 1, deep_rank.astype(F32), notes)
    for start, gate_ref in ((2, sgate_ref), (5, dgate_ref)):
        for at, piece in enumerate(split3(to_column(gate_ref[...], rows))):
            notes = jnp.where(lane == start + at, piece, notes)
    notes = jnp.where(lane == 8, 1.0, notes)
    full = jnp.concatenate([states, notes.astype(BF16)], axis=1)
    choose = (iota((EXPERTS * PAD, rows), 0) == to_row(place, rows)).astype(BF16)
    sent = dot(choose, full)
    for at, out in enumerate((out0, out1, out2, out3)):
        out[...] = sent[at * PAD : (at + 1) * PAD].astype(BF16)


def attend(arrays):
    rows, features = arrays[0].shape
    shape = jax.ShapeDtypeStruct((PAD, features + META), BF16)
    return pl.pallas_call(
        attend_kernel,
        in_specs=[HB] * len(arrays),
        out_specs=[VM] * 5,
        out_shape=[shape] * 4 + [jax.ShapeDtypeStruct((rows, META), jnp.int32)],
        scratch_shapes=[pltpu.VMEM(a.shape, a.dtype) for a in arrays]
        + [pltpu.SemaphoreType.DMA((len(arrays),))],
        compiler_params=params(16),
        name="attend",
    )(*[pltpu.with_memory_space_constraint(a, pltpu.HBM) for a in arrays])


def load_kernel(weight_ref, after_ref, out_ref, sems):
    count = sems.shape[0]
    rows = weight_ref.shape[0] // count
    copies = [
        pltpu.make_async_copy(
            weight_ref.at[pl.ds(i * rows, rows)], out_ref.at[pl.ds(i * rows, rows)], sems.at[i]
        )
        for i in range(count)
    ]
    for copy in copies:
        copy.start()
    for copy in copies:
        copy.wait()


def load(weights, after):
    return pl.pallas_call(
        load_kernel,
        in_specs=[HB, pl.BlockSpec(memory_space=pl.ANY)],
        out_specs=VM,
        out_shape=jax.ShapeDtypeStruct(weights.shape, weights.dtype),
        scratch_shapes=[pltpu.SemaphoreType.DMA((4,))],
        compiler_params=params(4),
        cost_estimate=cost(0, 2 * weights.size),
        name="load",
    )(pltpu.with_memory_space_constraint(weights, pltpu.HBM), after)


def choose_shallow():
    source = iota((TALL, EXPERTS * PAD), 1)
    kept = jnp.where(source % PAD < CAP, source // PAD * CAP + source % PAD, -1)
    return (kept == iota((TALL, EXPERTS * PAD), 0)).astype(BF16)


def choose_deep(here, held, features):
    notes = held[:, features:].astype(F32)
    count = held.shape[0]
    number = iota((count, 1), 0)
    apart = (number // SLOTS) ^ (number % SLOTS // CAP)
    place = apart * CAP + notes[:, 1:2].astype(jnp.int32)
    mine = (notes[:, 0:1].astype(jnp.int32) == here) & (notes[:, 8:9] > 0.5)
    place = jnp.where(mine, place, -1)
    return (iota((TALL, count), 0) == to_row(place, count)).astype(BF16)


def up_block(rows, means, weights):
    product = dot(rows, weights)
    columns = product[SLOTS : SLOTS + 1]
    row = iota(product.shape, 0)
    centred = product - means * columns
    return row, centred, columns


def cuts_of(half):
    unit = 4 * META
    first = max(unit, int(half * FIRST_SHARE) // unit * unit)
    return (0, first), (first, half - first)


def columns_at(weight_ref, own, at, step):
    half = weight_ref.shape[1] // 2
    which = core_here() if own else 1 - core_here()
    return weight_ref[:, pl.ds(pl.multiple_of(which * half + at, 128), step)]


def steps_of(width):
    return [(at, min(STEP, width - at)) for at in range(0, width, STEP)]


def up_first_kernel(deep, cuts, h0, h1, h2, h3, weight_ref, rows_ref, stats_ref, *sent):
    features = weight_ref.shape[0]
    held = jnp.concatenate([h0[...], h1[...], h2[...], h3[...]], axis=0)
    choose = choose_deep(lax.axis_index("ep"), held, features) if deep else choose_shallow()
    picked = dot(choose, held)
    ones = (iota(picked.shape, 0) == SLOTS) & (iota(picked.shape, 1) < features)
    rows_ref[...] = jnp.where(ones, 1.0, picked).astype(BF16)
    wide = picked[:, :features]
    lane = iota((TALL, META), 1)
    total = jnp.sum(wide, axis=1, keepdims=True)
    square = jnp.sum(wide * wide, axis=1, keepdims=True)
    stats_ref[...] = jnp.where(lane == 0, total, jnp.where(lane == 1, square, 0.0))
    means = total / features
    for (start, width), sent_ref in zip(cuts, sent):
        for at, step in steps_of(width):
            weights = columns_at(weight_ref, False, start + at, step)
            row, centred, columns = up_block(rows_ref[:, :features], means, weights)
            high = columns.astype(BF16).astype(F32)
            tail = jnp.where(row == SLOTS, high, jnp.where(row == SLOTS + 1, columns - high, 0.0))
            sent_ref[:, at : at + step] = jnp.where(row < SLOTS, centred, tail).astype(BF16)


def up_first(deep, cuts, held, weights):
    features, width = weights.shape
    half = width // 2
    return pl.pallas_call(
        functools.partial(up_first_kernel, deep, cuts),
        in_specs=[VM] * 5,
        out_specs=[VM] * 4,
        out_shape=[
            jax.ShapeDtypeStruct((TALL, features + META), BF16),
            jax.ShapeDtypeStruct((TALL, META), F32),
        ]
        + [jax.ShapeDtypeStruct((TALL, cut[1]), BF16) for cut in cuts],
        compiler_params=params(8),
        cost_estimate=cost(2 * TALL * features * half, 2 * features * half),
        name="up_first",
    )(*held, weights)


def up_second_kernel(start, rows_ref, stats_ref, weight_ref, kept_ref):
    features = weight_ref.shape[0]
    means = stats_ref[:, 0:1] / features
    for at, step in steps_of(kept_ref.shape[1]):
        weights = columns_at(weight_ref, True, start + at, step)
        row, centred, columns = up_block(rows_ref[:, :features], means, weights)
        kept_ref[:, at : at + step] = jnp.where(
            row < SLOTS, centred, jnp.where(row == SLOTS, columns, 0.0)
        )


def up_second(rows, stats, weights, cut):
    start, width = cut
    features = weights.shape[0]
    return pl.pallas_call(
        functools.partial(up_second_kernel, start),
        in_specs=[VM] * 3,
        out_specs=VM,
        out_shape=jax.ShapeDtypeStruct((TALL, width), F32),
        compiler_params=params(8),
        cost_estimate=cost(2 * TALL * features * width, 2 * features * width),
        name="up_second",
    )(rows, stats, weights)


def merge_into(features, source, width, got_ref, stats, other, sum_ref, sent_ref):
    apart = (stats[:, 0:1] - other[:, 0:1]) * (0.5 / features)
    held = jnp.zeros((SLOTS, META), F32)
    slot = iota((SLOTS, META), 0)
    for at, step in steps_of(width):
        kept = source(at, step)
        got = got_ref[:, at : at + step].astype(F32)
        mine = kept[SLOTS : SLOTS + 1]
        theirs = got[SLOTS : SLOTS + 1] + got[SLOTS + 1 : SLOTS + 2]
        row = iota(kept.shape, 0)
        columns = mine + theirs
        merged = jnp.where(row < SLOTS, kept + got + apart * (mine - theirs), columns)
        sum_ref[:, at : at + step] = merged
        sent_ref[:, at : at + step] = merged[:SLOTS].astype(BF16)
        for part in range(0, step, META):
            held = jnp.where(slot == (at + part) // META, columns[:, part : part + META], held)
    sent_ref[:, width : width + META] = held.astype(BF16)


def merge_kernel(features, kept_ref, got_ref, stats_ref, got_stats_ref, sent_ref, sum_ref, sums_ref):
    width = kept_ref.shape[1]
    stats, other = stats_ref[...], got_stats_ref[...]
    sums = stats + other
    sums_ref[...] = sums
    source = lambda at, step: kept_ref[:, at : at + step]
    merge_into(features, source, width, got_ref, stats, other, sum_ref, sent_ref)
    lane = iota((SLOTS, META), 1)
    packed = jnp.zeros((SLOTS, META), F32)
    for which in range(2):
        for at, piece in enumerate(split3(sums[:SLOTS, which : which + 1])):
            packed = jnp.where(lane == 3 * which + at, piece, packed)
    sent_ref[:, width + META :] = packed.astype(BF16)


def merge(features, kept, got, stats, got_stats):
    width = kept.shape[1]
    return pl.pallas_call(
        functools.partial(merge_kernel, features),
        in_specs=[VM] * 4,
        out_specs=[VM] * 3,
        out_shape=[
            jax.ShapeDtypeStruct((SLOTS, width + 2 * META), BF16),
            jax.ShapeDtypeStruct((TALL, width), F32),
            jax.ShapeDtypeStruct((TALL, META), F32),
        ],
        compiler_params=params(8),
        name="merge",
    )(kept, got, stats, got_stats)


def up_merge_kernel(
    start, rows_ref, stats_ref, got_stats_ref, weight_ref, got_ref, sent_ref, sum_ref
):
    features = weight_ref.shape[0]
    stats = stats_ref[...]
    means = stats[:, 0:1] / features

    def source(at, step):
        weights = columns_at(weight_ref, True, start + at, step)
        row, centred, columns = up_block(rows_ref[:, :features], means, weights)
        return jnp.where(row < SLOTS, centred, jnp.where(row == SLOTS, columns, 0.0))

    merge_into(features, source, sum_ref.shape[1], got_ref, stats, got_stats_ref[...], sum_ref, sent_ref)


def up_merge(rows, stats, got_stats, weights, got, cut):
    start, width = cut
    features = weights.shape[0]
    return pl.pallas_call(
        functools.partial(up_merge_kernel, start),
        in_specs=[VM] * 5,
        out_specs=[VM] * 2,
        out_shape=[
            jax.ShapeDtypeStruct((SLOTS, width + META), BF16),
            jax.ShapeDtypeStruct((TALL, width), F32),
        ],
        compiler_params=params(8),
        cost_estimate=cost(2 * TALL * features * width, 2 * features * width),
        name="up_merge",
    )(rows, stats, got_stats, weights, got)


def hidden_kernel(features, sum_ref, sums_ref, got_ref, packed_ref, hidden_ref):
    width = sum_ref.shape[1]
    packed = packed_ref[:, packed_ref.shape[1] - META :].astype(F32)
    held = got_ref[:, width : width + META].astype(F32)
    theirs_total = packed[:, 0:1] + packed[:, 1:2] + packed[:, 2:3]
    theirs_square = packed[:, 3:4] + packed[:, 4:5] + packed[:, 5:6]
    total, square = sums_ref[:SLOTS, 0:1], sums_ref[:SLOTS, 1:2]
    apart = (total - theirs_total) * (0.5 / (2 * features))
    center = (total + theirs_total) / D
    spread = (square + theirs_square) / D - center * center
    scale = lax.rsqrt(spread + epsilon)
    step = 4 * META
    for at in range(0, width, step):
        mine = sum_ref[:, at : at + step]
        got = got_ref[:, at : at + step].astype(F32)
        first = at // META
        theirs = jnp.concatenate([held[i : i + 1] for i in range(first, first + step // META)], axis=1)
        columns = mine[SLOTS : SLOTS + 1] - theirs
        pre = (mine[:SLOTS] + got + apart * columns) * scale
        hidden_ref[:, at : at + step] = jax.nn.gelu(pre, approximate=True).astype(BF16)


def hidden_units(features, total, sums, got, packed):
    return pl.pallas_call(
        functools.partial(hidden_kernel, features),
        in_specs=[VM] * 4,
        out_specs=VM,
        out_shape=jax.ShapeDtypeStruct((SLOTS, total.shape[1]), BF16),
        compiler_params=params(8),
        cost_estimate=cost(1, 1),
        name="hidden",
    )(total, sums, got, packed)


def rows_at(weight_ref, own, start, width):
    half = weight_ref.shape[0] // 2
    which = core_here() if own else 1 - core_here()
    return weight_ref[pl.ds(pl.multiple_of(which * half + start, 128), width), :]


def down_part_kernel(own, start, hidden_ref, weight_ref, *rest):
    *earlier, out_ref = rest
    product = dot(hidden_ref[...], rows_at(weight_ref, own, start, hidden_ref.shape[1]))
    for part in earlier:
        product = product + part[...]
    out_ref[...] = product


def down_part(hidden, weights, own, cut, *earlier):
    start, width = cut
    features = weights.shape[1]
    return pl.pallas_call(
        functools.partial(down_part_kernel, own, start),
        in_specs=[VM] * (2 + len(earlier)),
        out_specs=VM,
        out_shape=jax.ShapeDtypeStruct((SLOTS, features), F32),
        compiler_params=params(8),
        cost_estimate=cost(1, 1),
        name="down_part",
    )(hidden, weights, *earlier)


def down_last_kernel(deep, start, part_ref, rows_ref, hidden_ref, weight_ref, *outs):
    features = weight_ref.shape[1]
    weights = rows_at(weight_ref, False, start, hidden_ref.shape[1])
    total = part_ref[...] + dot(hidden_ref[...], weights)
    rows = rows_ref[...].astype(F32)[:SLOTS]
    notes = rows[:, features:]
    first = 5 if deep else 2
    gate = notes[:, first : first + 1] + notes[:, first + 1 : first + 2]
    gate = gate + notes[:, first + 2 : first + 3]
    result = rows[:, :features] + gate * total
    if not deep:
        outs[0][...] = jnp.concatenate([result, notes], axis=1).astype(BF16)
    else:
        target = iota((EXPERTS * PAD, SLOTS), 0)
        kept = jnp.where(target % PAD < CAP, target // PAD * CAP + target % PAD, -1)
        spread = (kept == iota((EXPERTS * PAD, SLOTS), 1)).astype(BF16)
        placed = dot(spread, result.astype(BF16))
        for at, out in enumerate(outs):
            out[...] = placed[at * PAD : (at + 1) * PAD].astype(BF16)


def down_last(deep, part, rows, hidden, weights, cut):
    start, width = cut
    features = weights.shape[1]
    shapes = [(PAD, features)] * EXPERTS if deep else [(SLOTS, features + META)]
    return pl.pallas_call(
        functools.partial(down_last_kernel, deep, start),
        in_specs=[VM] * 4,
        out_specs=[VM] * len(shapes),
        out_shape=[jax.ShapeDtypeStruct(shape, BF16) for shape in shapes],
        compiler_params=params(8),
        cost_estimate=cost(2 * SLOTS * features * width, 2 * features * width),
        name="down_last",
    )(part, rows, hidden, weights)


def finish_kernel(home_ref, g0, g1, g2, g3, out_ref):
    rows = out_ref.shape[0]
    choose = (iota((rows, EXPERTS * PAD), 1) == home_ref[:, 0:1]).astype(BF16)
    held = jnp.concatenate([g0[...], g1[...], g2[...], g3[...]], axis=0)
    out_ref[...] = dot(choose, held).astype(BF16)


def finish(home, got):
    return pl.pallas_call(
        finish_kernel,
        in_specs=[VM] * 5,
        out_specs=VM,
        out_shape=jax.ShapeDtypeStruct((home.shape[0], got[0].shape[1]), BF16),
        compiler_params=params(8),
        name="finish",
    )(home, *got)


def swap(value, axis, apart):
    count = lax.axis_size(axis)
    return lax.ppermute(value, axis, [(i, i ^ apart) for i in range(count)])


def swap_all(blocks):
    return [blocks[0]] + [swap(blocks[k], "ep", k) for k in (1, 2, 3)]


def after(value, earlier):
    return lax.optimization_barrier((value, earlier))[0]


def expert_block(deep, held, up, down):
    features, width = up.shape
    first, second = cuts = cuts_of(width // 2)
    rows, stats, sent_a, sent_b = up_first(deep, cuts, held, up)
    got_a, got_stats = swap(sent_a, "tp", 1), swap(stats, "tp", 1)
    got_b = swap(sent_b, "tp", 1)
    kept = up_second(rows, stats, up, first)
    sent_a, total_a, sums = merge(features, kept, got_a, stats, got_stats)
    over_a = swap(sent_a, "tp", 2)
    later = after(rows, sent_a)
    sent_b, total_b = up_merge(later, stats, got_stats, up, got_b, second)
    over_b = swap(sent_b, "tp", 2)
    hidden_a = hidden_units(features, after(total_a, sent_b), sums, over_a, over_a)
    other_a = swap(hidden_a, "tp", 1)
    part = down_part(hidden_a, down, True, first)
    part = down_part(other_a, down, False, first, part)
    hidden_b = hidden_units(features, after(total_b, part), sums, over_b, over_a)
    other_b = swap(hidden_b, "tp", 1)
    part = down_part(hidden_b, down, True, second, part)
    return down_last(deep, part, rows, other_b, down, second)


def fast_body(
    resid,
    query,
    new_key,
    new_value,
    cache_keys,
    cache_values,
    cache_lengths,
    shallow_expert,
    shallow_gate,
    shallow_up,
    shallow_down,
    deep_expert,
    deep_gate,
    deep_up,
    deep_down,
):
    rows = resid.shape[0]
    *blocks, home = attend(
        (
            resid,
            query,
            new_key,
            new_value,
            cache_keys,
            cache_values,
            cache_lengths.reshape(1, rows),
            shallow_expert.reshape(1, rows),
            shallow_gate.reshape(1, rows),
            deep_expert.reshape(1, rows),
            deep_gate.reshape(1, rows),
        ),
    )
    weights = load(shallow_up, blocks[0])
    (between,) = expert_block(False, swap_all(blocks), weights, shallow_down)
    blocks = expert_block(True, swap_all([between] * EXPERTS), load(deep_up, between), deep_down)
    return finish(home, swap_all(blocks))


def solution(mesh):
    fits = mesh.shape["ep"] == EXPERTS and mesh.shape["tp"] == 4
    return jax.shard_map(
        fast_body if fits else general_body,
        mesh=mesh,
        in_specs=(
            P(("groups", "ep"), "tp"),
            P(("groups", "ep"), "tp"),
            P(("groups", "ep"), "tp"),
            P(("groups", "ep"), "tp"),
            P(("groups", "ep"), None, "tp"),
            P(("groups", "ep"), None, "tp"),
            P(("groups", "ep")),
            P(("groups", "ep"), None),
            P(("groups", "ep")),
            P("tp", "ep"),
            P("ep", "tp"),
            P(("groups", "ep"), None),
            P(("groups", "ep")),
            P("tp", "ep"),
            P("ep", "tp"),
        ),
        out_specs=P(("groups", "ep"), "tp"),
        check_vma=False,
    )
```

```python
import functools
import math

import jax
import jax.numpy as jnp
from jax import lax
from jax.experimental import pallas as pl
from jax.experimental.pallas import tpu as pltpu
from jax.sharding import PartitionSpec as P

D = 4096
HD = 128
EXPERTS = 4
CAP = 12


epsilon = 1e-05


def attention(resid, query, new_key, new_value, cache_keys, cache_values, cache_lengths):
    row_count, feature_count = resid.shape
    heads_here = feature_count // HD
    depth = cache_keys.shape[1]
    queries = query.reshape(row_count, heads_here, HD)
    own_keys = new_key.reshape(row_count, heads_here, HD)
    own_values = new_value.reshape(row_count, heads_here, HD)
    past_keys = cache_keys.reshape(row_count, depth, heads_here, HD)
    past_values = cache_values.reshape(row_count, depth, heads_here, HD)
    factor = 1.0 / math.sqrt(HD)
    cached = (
        jnp.einsum("rhd,rjhd->rhj", queries, past_keys, preferred_element_type=jnp.float32) * factor
    )
    own_score = (
        jnp.einsum("rhd,rhd->rh", queries, own_keys, preferred_element_type=jnp.float32) * factor
    )
    valid = jnp.arange(depth)[None, None, :] < cache_lengths[:, None, None]
    masked = jnp.where(valid, cached, -1e30)
    highest = jnp.maximum(jnp.max(masked, axis=-1), own_score)
    cached_exp = jnp.where(valid, jnp.exp(masked - highest[..., None]), 0.0)
    own_exp = jnp.exp(own_score - highest)
    total = jnp.sum(cached_exp, axis=-1) + own_exp
    past_weights = (cached_exp / total[..., None]).astype(jnp.bfloat16)
    own_weight = (own_exp / total).astype(jnp.bfloat16)
    attended = jnp.einsum(
        "rhj,rjhd->rhd", past_weights, past_values, preferred_element_type=jnp.float32
    )
    attended = attended + own_weight.astype(jnp.float32)[..., None] * own_values.astype(jnp.float32)
    return (resid.astype(jnp.float32) + attended.reshape(row_count, feature_count)).astype(
        jnp.bfloat16
    )


def expert_layer(states, expert_ids, gates, up_weight, down_weight):
    row_count, feature_count = states.shape
    ep_count = lax.axis_size("ep")
    sharing = ep_count // EXPERTS
    mine = lax.axis_index("ep") // sharing
    wide = states.astype(jnp.float32)
    row_sum, row_square = lax.psum((jnp.sum(wide, axis=1), jnp.sum(wide * wide, axis=1)), "tp")
    center = row_sum / D
    spread = row_square / D - center * center
    normalized = ((wide - center[:, None]) * lax.rsqrt(spread + epsilon)[:, None]).astype(
        jnp.bfloat16
    )
    slots = CAP
    routed = expert_ids[:, 0]
    onehot = (routed[:, None] == jnp.arange(EXPERTS)[None, :]).astype(jnp.int32)
    earlier = jnp.cumsum(onehot, axis=0) - onehot
    rank_in = jnp.sum(earlier * onehot, axis=1)
    position = routed * slots + rank_in
    placing = (position[None, :] == jnp.arange(EXPERTS * slots)[:, None]).astype(jnp.bfloat16)
    compact = jnp.dot(placing, normalized, preferred_element_type=jnp.float32).astype(jnp.bfloat16)
    compact = compact.reshape(EXPERTS, slots, feature_count)
    chosen = lax.dynamic_index_in_dim(
        lax.all_gather(compact[None], "ep", axis=0, tiled=True), mine, axis=1, keepdims=False
    )
    pre = jnp.einsum("scd,df->scf", chosen, up_weight, preferred_element_type=jnp.float32)
    hidden_width = pre.shape[2]
    flat_pre = pre.reshape(ep_count * slots, hidden_width)
    summed = lax.psum(flat_pre, "tp")
    activated = jax.nn.gelu(summed, approximate=True).astype(jnp.bfloat16)
    partial_value = jnp.dot(activated, down_weight, preferred_element_type=jnp.float32)
    returned = lax.all_to_all(
        partial_value.reshape(ep_count, slots, feature_count),
        "ep",
        split_axis=0,
        concat_axis=0,
        tiled=True,
    )
    combined = jnp.sum(returned.reshape(EXPERTS, sharing, slots, feature_count), axis=1)
    combined = combined.reshape(EXPERTS * slots, feature_count)
    produced = jnp.take(combined, position, axis=0)
    return (wide + gates[:, None] * produced).astype(jnp.bfloat16)


def general_body(
    resid,
    query,
    new_key,
    new_value,
    cache_keys,
    cache_values,
    cache_lengths,
    shallow_expert,
    shallow_gate,
    shallow_up,
    shallow_down,
    deep_expert,
    deep_gate,
    deep_up,
    deep_down,
):
    shallow_in = attention(
        resid, query, new_key, new_value, cache_keys, cache_values, cache_lengths
    )
    shallow_out = expert_layer(shallow_in, shallow_expert, shallow_gate, shallow_up, shallow_down)
    return expert_layer(shallow_out, deep_expert, deep_gate, deep_up, deep_down)


SLOTS = EXPERTS * CAP
PAD = 16
TALL = 56
META = 128
MIB = 1 << 20
STEP = 1024
FIRST_SHARE = 0.5625
F32 = jnp.float32
BF16 = jnp.bfloat16


def iota(shape, dim):
    return lax.broadcasted_iota(jnp.int32, shape, dim)


def to_column(row, count):
    same = iota((count, count), 0) == iota((count, count), 1)
    return jnp.sum(jnp.where(same, row, jnp.zeros_like(row)), axis=1, keepdims=True)


def to_row(column, count):
    same = iota((count, count), 0) == iota((count, count), 1)
    return jnp.sum(jnp.where(same, column, jnp.zeros_like(column)), axis=0, keepdims=True)


def ranks(id_row, id_column, count):
    earlier = iota((count, count), 1) < iota((count, count), 0)
    same = (id_row == id_column) & earlier
    return jnp.sum(same.astype(jnp.int32), axis=1, keepdims=True)


def split3(value):
    high = value.astype(BF16).astype(F32)
    middle = (value - high).astype(BF16).astype(F32)
    low = (value - high - middle).astype(BF16).astype(F32)
    return high, middle, low


def core_here():
    return lax.axis_index("tp") & 1


def dot(left, right):
    return jnp.dot(left, right, preferred_element_type=F32)


def params(mib):
    return pltpu.CompilerParams(vmem_limit_bytes=mib * MIB)


def cost(flops, moved):
    return pl.CostEstimate(flops=flops, bytes_accessed=moved, transcendentals=0)


VM = pl.BlockSpec(memory_space=pltpu.VMEM)
HB = pl.BlockSpec(memory_space=pltpu.HBM)


def attend_kernel(
    resid_in, query_in, key_in, value_in, keys_in, values_in, length_in,
    shallow_in, sgate_in, deep_in, dgate_in, out0, out1, out2, out3, home_ref,
    resid_ref, query_ref, key_ref, value_ref, keys_ref, values_ref, length_ref,
    shallow_ref, sgate_ref, deep_ref, dgate_ref, sems,
):
    rows, features = resid_ref.shape
    depth = keys_ref.shape[1]
    flat = rows * depth
    factor = 1.0 / math.sqrt(HD)
    order = (
        (query_in, query_ref), (keys_in, keys_ref), (key_in, key_ref), (length_in, length_ref),
        (values_in, values_ref), (value_in, value_ref), (resid_in, resid_ref),
        (shallow_in, shallow_ref), (sgate_in, sgate_ref), (deep_in, deep_ref), (dgate_in, dgate_ref),
    )
    copies = [pltpu.make_async_copy(a, b, sems.at[i]) for i, (a, b) in enumerate(order)]
    for copy in copies:
        copy.start()
    spread = (iota((features, META), 0) // HD == iota((features, META), 1)).astype(BF16)
    gather = (iota((META, features), 1) // HD == iota((META, features), 0)).astype(BF16)

    def head_sums(products):
        high = products.astype(BF16)
        low = (products - high.astype(F32)).astype(BF16)
        return dot(high, spread) + dot(low, spread)

    for copy in copies[:4]:
        copy.wait()
    query = query_ref[...].astype(F32)
    own = head_sums(query * key_ref[...].astype(F32)) * factor
    products = query[:, None, :] * keys_ref[...].astype(F32)
    cached = head_sums(products.reshape(flat, features)) * factor
    repeated = iota((flat, rows), 0) // depth == iota((flat, rows), 1)
    length = jnp.sum(jnp.where(repeated, length_ref[...], 0), axis=1, keepdims=True)
    valid = (iota((flat, META), 0) % depth) < length
    masked = jnp.where(valid, cached, -1e30).reshape(rows, depth, META)
    highest = jnp.maximum(jnp.max(masked, axis=1), own)
    past = jnp.exp(masked - highest[:, None, :])
    past = jnp.where(valid, past.reshape(flat, META), 0.0).reshape(rows, depth, META)
    own_exp = jnp.exp(own - highest)
    total = jnp.sum(past, axis=1) + own_exp
    weights = (past / total[:, None, :]).reshape(flat, META).astype(BF16)
    own_weight = (own_exp / total).astype(BF16)
    for copy in copies[4:]:
        copy.wait()
    wide = dot(weights, gather).reshape(rows, depth, features)
    attended = jnp.sum(wide * values_ref[...].astype(F32), axis=1)
    attended = attended + dot(own_weight, gather) * value_ref[...].astype(F32)
    states = (resid_ref[...].astype(F32) + attended).astype(BF16)

    here = lax.axis_index("ep")
    shallow = shallow_ref[...]
    deep = deep_ref[...]
    shallow_column = to_column(shallow, rows)
    deep_column = to_column(deep, rows)
    shallow_rank = ranks(shallow, shallow_column, rows)
    deep_rank = ranks(deep, deep_column, rows)
    place = (shallow_column ^ here) * PAD + shallow_rank
    home_ref[...] = jnp.broadcast_to((deep_column ^ here) * PAD + deep_rank, (rows, META))
    choose = (iota((EXPERTS * PAD, rows), 0) == to_row(place, rows)).astype(BF16)
    sent = dot(choose, states)
    lane = iota((rows, META), 1)
    shallow_gates = split3(to_column(sgate_ref[...], rows))
    deep_gates = split3(to_column(dgate_ref[...], rows))
    row = iota((PAD, META), 0)
    for at, out in enumerate((out0, out1, out2, out3)):
        to_shallow = (shallow_column == here ^ at) & (lane == shallow_rank)
        to_deep = (deep_column == here ^ at) & (lane == deep_rank)
        line = lambda kept, value: jnp.sum(jnp.where(kept, value, 0.0), axis=0, keepdims=True)
        apart = shallow_column ^ deep_column
        source = (apart * SLOTS + (shallow_column ^ here) * CAP + shallow_rank + 1).astype(F32)
        block = sent[at * PAD : (at + 1) * PAD]
        pieces = []
        for part in range(3):
            note = jnp.where(row == CAP, line(to_shallow, shallow_gates[part]), block[:, part * META : (part + 1) * META])
            note = jnp.where(row == CAP + 1, line(to_deep, deep_gates[part]), note)
            if part == 0:
                note = jnp.where(row == CAP + 2, line(to_deep, source), note)
            pieces.append(note)
        block = jnp.concatenate(pieces + [block[:, 3 * META :]], axis=1)
        out[...] = block.astype(BF16)


def attend(arrays):
    rows, features = arrays[0].shape
    shape = jax.ShapeDtypeStruct((PAD, features), BF16)
    return pl.pallas_call(
        attend_kernel,
        in_specs=[HB] * len(arrays),
        out_specs=[VM] * 5,
        out_shape=[shape] * 4 + [jax.ShapeDtypeStruct((rows, META), jnp.int32)],
        scratch_shapes=[pltpu.VMEM(a.shape, a.dtype) for a in arrays]
        + [pltpu.SemaphoreType.DMA((len(arrays),))],
        compiler_params=params(16),
        name="attend",
    )(*[pltpu.with_memory_space_constraint(a, pltpu.HBM) for a in arrays])


def load_kernel(weight_ref, after_ref, out_ref, sems):
    count = sems.shape[0]
    rows = weight_ref.shape[0] // count
    copies = [
        pltpu.make_async_copy(
            weight_ref.at[pl.ds(i * rows, rows)], out_ref.at[pl.ds(i * rows, rows)], sems.at[i]
        )
        for i in range(count)
    ]
    for copy in copies:
        copy.start()
    for copy in copies:
        copy.wait()


def load(weights, after):
    return pl.pallas_call(
        load_kernel,
        in_specs=[HB, pl.BlockSpec(memory_space=pl.ANY)],
        out_specs=VM,
        out_shape=jax.ShapeDtypeStruct(weights.shape, weights.dtype),
        scratch_shapes=[pltpu.SemaphoreType.DMA((4,))],
        compiler_params=params(4),
        cost_estimate=cost(0, 2 * weights.size),
        name="load",
    )(pltpu.with_memory_space_constraint(weights, pltpu.HBM), after)


def choose_shallow():
    source = iota((TALL, EXPERTS * PAD), 1)
    kept = jnp.where(source % PAD < CAP, source // PAD * CAP + source % PAD, -1)
    return (kept == iota((TALL, EXPERTS * PAD), 0)).astype(BF16)


def notes_of(held):
    slot, lane = iota((TALL, META), 0), iota((TALL, META), 1)
    columns = []
    for row in range(CAP, CAP + 3):
        column = jnp.zeros((TALL, 1), F32)
        for at in range(EXPERTS):
            line = held[at * PAD + row : at * PAD + row + 1]
            value = line[:, :META]
            if row < CAP + 2:
                value = value + line[:, META : 2 * META] + line[:, 2 * META : 3 * META]
            kept = (slot - at * CAP == lane) & (lane < CAP)
            column = column + jnp.sum(jnp.where(kept, value, 0.0), axis=1, keepdims=True)
        columns.append(column)
    notes = jnp.where(lane == 0, columns[0], 0.0)
    notes = jnp.where(lane == 1, columns[1], notes)
    return jnp.where(lane == 2, columns[2], notes)


def up_block(rows, means, weights):
    product = dot(rows, weights)
    columns = product[SLOTS : SLOTS + 1]
    row = iota(product.shape, 0)
    centred = product - means * columns
    return row, centred, columns


def cuts_of(half):
    unit = 2 * META
    first = max(unit, int(half * FIRST_SHARE) // unit * unit)
    return (0, first), (first, half - first)


def columns_at(weight_ref, own, at, step):
    half = weight_ref.shape[1] // 2
    which = core_here() if own else 1 - core_here()
    return weight_ref[:, pl.ds(pl.multiple_of(which * half + at, 128), step)]


def steps_of(width):
    return [(at, min(STEP, width - at)) for at in range(0, width, STEP)]


def send_block(rows_ref, means, weight_ref, start, sent_ref):
    for at, step in steps_of(sent_ref.shape[1]):
        weights = columns_at(weight_ref, False, start + at, step)
        row, centred, columns = up_block(rows_ref[...], means, weights)
        high = columns.astype(BF16).astype(F32)
        tail = jnp.where(row == SLOTS, high, jnp.where(row == SLOTS + 1, columns - high, 0.0))
        sent_ref[:, at : at + step] = jnp.where(row < SLOTS, centred, tail).astype(BF16)


def up_first_kernel(deep, start, *refs):
    if deep:
        notes_ref, h0, h1, h2, h3, weight_ref, rows_ref, stats_ref, sent_ref = refs
    else:
        h0, h1, h2, h3, weight_ref, rows_ref, stats_ref, sent_ref, notes_ref = refs
    held = jnp.concatenate([h0[...], h1[...], h2[...], h3[...]], axis=0)
    if deep:
        place = notes_ref[:, 2:3].astype(jnp.int32) - 1
        choose = (iota((TALL, held.shape[0]), 1) == place).astype(BF16)
    else:
        choose = choose_shallow()
        notes_ref[...] = notes_of(held.astype(F32))
    wide = dot(choose, held)
    rows_ref[...] = jnp.where(iota(wide.shape, 0) == SLOTS, 1.0, wide).astype(BF16)
    features = wide.shape[1]
    lane = iota((TALL, META), 1)
    total = jnp.sum(wide, axis=1, keepdims=True)
    square = jnp.sum(wide * wide, axis=1, keepdims=True)
    stats_ref[...] = jnp.where(lane == 0, total, jnp.where(lane == 1, square, 0.0))
    send_block(rows_ref, total / features, weight_ref, start, sent_ref)


def up_first(deep, cut, notes, held, weights):
    features = weights.shape[0]
    start, width = cut
    operands = ([notes] if deep else []) + list(held)
    note = jax.ShapeDtypeStruct((TALL, META), F32)
    out = pl.pallas_call(
        functools.partial(up_first_kernel, deep, start),
        in_specs=[VM] * (len(operands) + 1),
        out_specs=[VM] * (3 if deep else 4),
        out_shape=[
            jax.ShapeDtypeStruct((TALL, features), BF16),
            note,
            jax.ShapeDtypeStruct((TALL, width), BF16),
        ]
        + ([] if deep else [note]),
        compiler_params=params(8),
        cost_estimate=cost(2 * TALL * features * width, 2 * features * width),
        name="up_first",
    )(*operands, weights)
    return out if not deep else [*out, notes]


def up_other_kernel(start, rows_ref, stats_ref, weight_ref, *sent):
    for sent_ref in sent:
        send_block(rows_ref, stats_ref[:, 0:1] / rows_ref.shape[1], weight_ref, start, sent_ref)
        start += sent_ref.shape[1]


def up_other(rows, stats, weights, cut):
    start, width = cut
    features = weights.shape[0]
    return pl.pallas_call(
        functools.partial(up_other_kernel, start),
        in_specs=[VM] * 3,
        out_specs=[VM] * 2,
        out_shape=[jax.ShapeDtypeStruct((TALL, width // 2), BF16)] * 2,
        compiler_params=params(8),
        cost_estimate=cost(2 * TALL * features * width, 2 * features * width),
        name="up_other",
    )(rows, stats, weights)


def up_second_kernel(start, rows_ref, stats_ref, weight_ref, kept_ref):
    features = weight_ref.shape[0]
    means = stats_ref[:, 0:1] / features
    for at, step in steps_of(kept_ref.shape[1]):
        weights = columns_at(weight_ref, True, start + at, step)
        row, centred, columns = up_block(rows_ref[...], means, weights)
        kept_ref[:, at : at + step] = jnp.where(
            row < SLOTS, centred, jnp.where(row == SLOTS, columns, 0.0)
        )


def up_second(rows, stats, weights, cut):
    start, width = cut
    features = weights.shape[0]
    return pl.pallas_call(
        functools.partial(up_second_kernel, start),
        in_specs=[VM] * 3,
        out_specs=VM,
        out_shape=jax.ShapeDtypeStruct((TALL, width), F32),
        compiler_params=params(8),
        cost_estimate=cost(2 * TALL * features * width, 2 * features * width),
        name="up_second",
    )(rows, stats, weights)


def merge_into(features, source, width, got_refs, stats, other, sum_ref, sent_ref):
    apart = (stats[:, 0:1] - other[:, 0:1]) * (0.5 / features)
    held = jnp.zeros((SLOTS, META), F32)
    slot = iota((SLOTS, META), 0)
    span = width // len(got_refs)
    pieces = [(ref, i * span, at, step) for i, ref in enumerate(got_refs) for at, step in steps_of(span)]
    for got_ref, base, start, step in pieces:
        at = base + start
        kept = source(at, step)
        got = got_ref[:, start : start + step].astype(F32)
        mine = kept[SLOTS : SLOTS + 1]
        theirs = got[SLOTS : SLOTS + 1] + got[SLOTS + 1 : SLOTS + 2]
        row = iota(kept.shape, 0)
        columns = mine + theirs
        merged = jnp.where(row < SLOTS, kept + got + apart * (mine - theirs), columns)
        sum_ref[:, at : at + step] = merged
        sent_ref[:, at : at + step] = merged[:SLOTS].astype(BF16)
        for part in range(0, step, META):
            held = jnp.where(slot == (at + part) // META, columns[:, part : part + META], held)
    sent_ref[:, width : width + META] = held.astype(BF16)


def merge_kernel(features, kept_ref, got_ref, stats_ref, got_stats_ref, sent_ref, sum_ref, sums_ref):
    width = kept_ref.shape[1]
    stats, other = stats_ref[...], got_stats_ref[...]
    sums = stats + other
    sums_ref[...] = sums
    source = lambda at, step: kept_ref[:, at : at + step]
    merge_into(features, source, width, [got_ref], stats, other, sum_ref, sent_ref)
    lane = iota((SLOTS, META), 1)
    packed = jnp.zeros((SLOTS, META), F32)
    for which in range(2):
        for at, piece in enumerate(split3(sums[:SLOTS, which : which + 1])):
            packed = jnp.where(lane == 3 * which + at, piece, packed)
    sent_ref[:, width + META :] = packed.astype(BF16)


def merge(features, kept, got, stats, got_stats):
    width = kept.shape[1]
    return pl.pallas_call(
        functools.partial(merge_kernel, features),
        in_specs=[VM] * 4,
        out_specs=[VM] * 3,
        out_shape=[
            jax.ShapeDtypeStruct((SLOTS, width + 2 * META), BF16),
            jax.ShapeDtypeStruct((TALL, width), F32),
            jax.ShapeDtypeStruct((TALL, META), F32),
        ],
        compiler_params=params(8),
        name="merge",
    )(kept, got, stats, got_stats)


def up_merge_kernel(
    start, rows_ref, stats_ref, got_stats_ref, weight_ref, got0, got1, sent_ref, sum_ref
):
    features = weight_ref.shape[0]
    stats = stats_ref[...]
    means = stats[:, 0:1] / features

    def source(at, step):
        weights = columns_at(weight_ref, True, start + at, step)
        row, centred, columns = up_block(rows_ref[...], means, weights)
        return jnp.where(row < SLOTS, centred, jnp.where(row == SLOTS, columns, 0.0))

    got = [got0, got1]
    merge_into(features, source, sum_ref.shape[1], got, stats, got_stats_ref[...], sum_ref, sent_ref)


def up_merge(rows, stats, got_stats, weights, got, cut):
    start, width = cut
    features = weights.shape[0]
    return pl.pallas_call(
        functools.partial(up_merge_kernel, start),
        in_specs=[VM] * 6,
        out_specs=[VM] * 2,
        out_shape=[
            jax.ShapeDtypeStruct((SLOTS, width + META), BF16),
            jax.ShapeDtypeStruct((TALL, width), F32),
        ],
        compiler_params=params(8),
        cost_estimate=cost(2 * TALL * features * width, 2 * features * width),
        name="up_merge",
    )(rows, stats, got_stats, weights, *got)


def hidden_kernel(features, sum_ref, sums_ref, got_ref, packed_ref, *hidden):
    width = sum_ref.shape[1]
    packed = packed_ref[:, packed_ref.shape[1] - META :].astype(F32)
    held = got_ref[:, width : width + META].astype(F32)
    theirs_total = packed[:, 0:1] + packed[:, 1:2] + packed[:, 2:3]
    theirs_square = packed[:, 3:4] + packed[:, 4:5] + packed[:, 5:6]
    total, square = sums_ref[:SLOTS, 0:1], sums_ref[:SLOTS, 1:2]
    apart = (total - theirs_total) * (0.5 / (2 * features))
    center = (total + theirs_total) / D
    spread = (square + theirs_square) / D - center * center
    scale = lax.rsqrt(spread + epsilon)
    span = width // len(hidden)
    pieces = [(ref, i * span, at, step) for i, ref in enumerate(hidden) for at, step in steps_of(span)]
    for hidden_ref, base, start, step in pieces:
        at = base + start
        mine = sum_ref[:, at : at + step]
        got = got_ref[:, at : at + step].astype(F32)
        first = at // META
        theirs = jnp.concatenate([held[i : i + 1] for i in range(first, first + step // META)], axis=1)
        columns = mine[SLOTS : SLOTS + 1] - theirs
        pre = (mine[:SLOTS] + got + apart * columns) * scale
        hidden_ref[:, start : start + step] = jax.nn.gelu(pre, approximate=True).astype(BF16)


def hidden_units(features, total, sums, got, packed, count):
    return pl.pallas_call(
        functools.partial(hidden_kernel, features),
        in_specs=[VM] * 4,
        out_specs=[VM] * count,
        out_shape=[jax.ShapeDtypeStruct((SLOTS, total.shape[1] // count), BF16)] * count,
        compiler_params=params(8),
        cost_estimate=cost(1, 1),
        name="hidden",
    )(total, sums, got, packed)


def rows_at(weight_ref, own, start, width):
    half = weight_ref.shape[0] // 2
    which = core_here() if own else 1 - core_here()
    return weight_ref[pl.ds(pl.multiple_of(which * half + start, 128), width), :]


def down_part_kernel(own, start, count, weight_ref, *refs):
    hidden, earlier, out_ref = refs[:count], refs[count:-1], refs[-1]
    product = None
    for part in hidden:
        width = part.shape[1]
        term = dot(part[...], rows_at(weight_ref, own, start, width))
        product = term if product is None else product + term
        start += width
    for part in earlier:
        product = product + part[...]
    out_ref[...] = product


def down_part(hidden, weights, own, cut, *earlier):
    features = weights.shape[1]
    return pl.pallas_call(
        functools.partial(down_part_kernel, own, cut[0], len(hidden)),
        in_specs=[VM] * (1 + len(hidden) + len(earlier)),
        out_specs=VM,
        out_shape=jax.ShapeDtypeStruct((SLOTS, features), F32),
        compiler_params=params(8),
        cost_estimate=cost(1, 1),
        name="down_part",
    )(weights, *hidden, *earlier)


def down_last_kernel(deep, start, part_ref, rows_ref, notes_ref, hidden_ref, weight_ref, *outs):
    features = weight_ref.shape[1]
    weights = rows_at(weight_ref, False, start, hidden_ref.shape[1])
    total = part_ref[...] + dot(hidden_ref[...], weights)
    which = 1 if deep else 0
    gate = notes_ref[:SLOTS, which : which + 1]
    result = rows_ref[...].astype(F32)[:SLOTS] + gate * total
    if not deep:
        outs[0][...] = result.astype(BF16)
    else:
        target = iota((EXPERTS * PAD, SLOTS), 0)
        kept = jnp.where(target % PAD < CAP, target // PAD * CAP + target % PAD, -1)
        spread = (kept == iota((EXPERTS * PAD, SLOTS), 1)).astype(BF16)
        placed = dot(spread, result.astype(BF16))
        for at, out in enumerate(outs):
            out[...] = placed[at * PAD : (at + 1) * PAD].astype(BF16)


def down_last(deep, part, rows, notes, hidden, weights, cut):
    start, width = cut
    features = weights.shape[1]
    shapes = [(PAD, features)] * EXPERTS if deep else [(SLOTS, features)]
    return pl.pallas_call(
        functools.partial(down_last_kernel, deep, start),
        in_specs=[VM] * 5,
        out_specs=[VM] * len(shapes),
        out_shape=[jax.ShapeDtypeStruct(shape, BF16) for shape in shapes],
        compiler_params=params(8),
        cost_estimate=cost(2 * SLOTS * features * width, 2 * features * width),
        name="down_last",
    )(part, rows, notes, hidden, weights)


def finish_kernel(home_ref, g0, g1, g2, g3, out_ref):
    rows = out_ref.shape[0]
    choose = (iota((rows, EXPERTS * PAD), 1) == home_ref[:, 0:1]).astype(BF16)
    held = jnp.concatenate([g0[...], g1[...], g2[...], g3[...]], axis=0)
    out_ref[...] = dot(choose, held).astype(BF16)


def finish(home, got):
    return pl.pallas_call(
        finish_kernel,
        in_specs=[VM] * 5,
        out_specs=VM,
        out_shape=jax.ShapeDtypeStruct((home.shape[0], got[0].shape[1]), BF16),
        compiler_params=params(8),
        name="finish",
    )(home, *got)


def swap(value, axis, apart):
    count = lax.axis_size(axis)
    return lax.ppermute(value, axis, [(i, i ^ apart) for i in range(count)])


def swap_all(blocks):
    return [blocks[0]] + [swap(blocks[k], "ep", k) for k in (1, 2, 3)]


def after(value, earlier):
    return lax.optimization_barrier((value, earlier))[0]


def expert_block(deep, notes, held, up, down):
    features, width = up.shape
    first, second = cuts_of(width // 2)
    rows, stats, sent_a, notes = up_first(deep, first, notes, held, up)
    got_a, got_stats = swap(sent_a, "tp", 1), swap(stats, "tp", 1)
    kept = up_second(rows, stats, up, first)
    sent_a, total_a, sums = merge(features, kept, got_a, stats, got_stats)
    over_a = swap(sent_a, "tp", 2)
    later = after(rows, sent_a)
    got_b = [swap(sent, "tp", 1) for sent in up_other(later, stats, up, second)]
    sent_b, total_b = up_merge(later, stats, got_stats, up, got_b, second)
    over_b = swap(sent_b, "tp", 2)
    hidden_a = hidden_units(features, after(total_a, sent_b), sums, over_a, over_a, 2)
    other_a = [swap(hidden, "tp", 1) for hidden in hidden_a]
    part = down_part(hidden_a, down, True, first)
    part = down_part(other_a, down, False, first, part)
    (hidden_b,) = hidden_units(features, after(total_b, part), sums, over_b, over_a, 1)
    other_b = swap(hidden_b, "tp", 1)
    part = down_part([hidden_b], down, True, second, part)
    return notes, down_last(deep, part, rows, notes, other_b, down, second)


def fast_body(
    resid,
    query,
    new_key,
    new_value,
    cache_keys,
    cache_values,
    cache_lengths,
    shallow_expert,
    shallow_gate,
    shallow_up,
    shallow_down,
    deep_expert,
    deep_gate,
    deep_up,
    deep_down,
):
    rows = resid.shape[0]
    *blocks, home = attend(
        (
            resid,
            query,
            new_key,
            new_value,
            cache_keys,
            cache_values,
            cache_lengths.reshape(1, rows),
            shallow_expert.reshape(1, rows),
            shallow_gate.reshape(1, rows),
            deep_expert.reshape(1, rows),
            deep_gate.reshape(1, rows),
        ),
    )
    weights = load(shallow_up, blocks[0])
    notes, (between,) = expert_block(False, None, swap_all(blocks), weights, shallow_down)
    _, blocks = expert_block(True, notes, swap_all([between] * EXPERTS), load(deep_up, between), deep_down)
    return finish(home, swap_all(blocks))


def solution(mesh):
    fits = mesh.shape["ep"] == EXPERTS and mesh.shape["tp"] == 4
    return jax.shard_map(
        fast_body if fits else general_body,
        mesh=mesh,
        in_specs=(
            P(("groups", "ep"), "tp"),
            P(("groups", "ep"), "tp"),
            P(("groups", "ep"), "tp"),
            P(("groups", "ep"), "tp"),
            P(("groups", "ep"), None, "tp"),
            P(("groups", "ep"), None, "tp"),
            P(("groups", "ep")),
            P(("groups", "ep"), None),
            P(("groups", "ep")),
            P("tp", "ep"),
            P("ep", "tp"),
            P(("groups", "ep"), None),
            P(("groups", "ep")),
            P("tp", "ep"),
            P("ep", "tp"),
        ),
        out_specs=P(("groups", "ep"), "tp"),
        check_vma=False,
    )
```

```python
import functools
import math

import jax
import jax.numpy as jnp
from jax import lax
from jax.experimental import pallas as pl
from jax.experimental.pallas import tpu as pltpu
from jax.sharding import PartitionSpec as P

D = 4096
HD = 128
EXPERTS = 4
CAP = 12


epsilon = 1e-05


def attention(resid, query, new_key, new_value, cache_keys, cache_values, cache_lengths):
    row_count, feature_count = resid.shape
    heads_here = feature_count // HD
    depth = cache_keys.shape[1]
    queries = query.reshape(row_count, heads_here, HD)
    own_keys = new_key.reshape(row_count, heads_here, HD)
    own_values = new_value.reshape(row_count, heads_here, HD)
    past_keys = cache_keys.reshape(row_count, depth, heads_here, HD)
    past_values = cache_values.reshape(row_count, depth, heads_here, HD)
    factor = 1.0 / math.sqrt(HD)
    cached = (
        jnp.einsum("rhd,rjhd->rhj", queries, past_keys, preferred_element_type=jnp.float32) * factor
    )
    own_score = (
        jnp.einsum("rhd,rhd->rh", queries, own_keys, preferred_element_type=jnp.float32) * factor
    )
    valid = jnp.arange(depth)[None, None, :] < cache_lengths[:, None, None]
    masked = jnp.where(valid, cached, -1e30)
    highest = jnp.maximum(jnp.max(masked, axis=-1), own_score)
    cached_exp = jnp.where(valid, jnp.exp(masked - highest[..., None]), 0.0)
    own_exp = jnp.exp(own_score - highest)
    total = jnp.sum(cached_exp, axis=-1) + own_exp
    past_weights = (cached_exp / total[..., None]).astype(jnp.bfloat16)
    own_weight = (own_exp / total).astype(jnp.bfloat16)
    attended = jnp.einsum(
        "rhj,rjhd->rhd", past_weights, past_values, preferred_element_type=jnp.float32
    )
    attended = attended + own_weight.astype(jnp.float32)[..., None] * own_values.astype(jnp.float32)
    return (resid.astype(jnp.float32) + attended.reshape(row_count, feature_count)).astype(
        jnp.bfloat16
    )


def expert_layer(states, expert_ids, gates, up_weight, down_weight):
    row_count, feature_count = states.shape
    ep_count = lax.axis_size("ep")
    sharing = ep_count // EXPERTS
    mine = lax.axis_index("ep") // sharing
    wide = states.astype(jnp.float32)
    row_sum, row_square = lax.psum((jnp.sum(wide, axis=1), jnp.sum(wide * wide, axis=1)), "tp")
    center = row_sum / D
    spread = row_square / D - center * center
    normalized = ((wide - center[:, None]) * lax.rsqrt(spread + epsilon)[:, None]).astype(
        jnp.bfloat16
    )
    slots = CAP
    routed = expert_ids[:, 0]
    onehot = (routed[:, None] == jnp.arange(EXPERTS)[None, :]).astype(jnp.int32)
    earlier = jnp.cumsum(onehot, axis=0) - onehot
    rank_in = jnp.sum(earlier * onehot, axis=1)
    position = routed * slots + rank_in
    placing = (position[None, :] == jnp.arange(EXPERTS * slots)[:, None]).astype(jnp.bfloat16)
    compact = jnp.dot(placing, normalized, preferred_element_type=jnp.float32).astype(jnp.bfloat16)
    compact = compact.reshape(EXPERTS, slots, feature_count)
    chosen = lax.dynamic_index_in_dim(
        lax.all_gather(compact[None], "ep", axis=0, tiled=True), mine, axis=1, keepdims=False
    )
    pre = jnp.einsum("scd,df->scf", chosen, up_weight, preferred_element_type=jnp.float32)
    hidden_width = pre.shape[2]
    flat_pre = pre.reshape(ep_count * slots, hidden_width)
    summed = lax.psum(flat_pre, "tp")
    activated = jax.nn.gelu(summed, approximate=True).astype(jnp.bfloat16)
    partial_value = jnp.dot(activated, down_weight, preferred_element_type=jnp.float32)
    returned = lax.all_to_all(
        partial_value.reshape(ep_count, slots, feature_count),
        "ep",
        split_axis=0,
        concat_axis=0,
        tiled=True,
    )
    combined = jnp.sum(returned.reshape(EXPERTS, sharing, slots, feature_count), axis=1)
    combined = combined.reshape(EXPERTS * slots, feature_count)
    produced = jnp.take(combined, position, axis=0)
    return (wide + gates[:, None] * produced).astype(jnp.bfloat16)


def general_body(
    resid,
    query,
    new_key,
    new_value,
    cache_keys,
    cache_values,
    cache_lengths,
    shallow_expert,
    shallow_gate,
    shallow_up,
    shallow_down,
    deep_expert,
    deep_gate,
    deep_up,
    deep_down,
):
    shallow_in = attention(
        resid, query, new_key, new_value, cache_keys, cache_values, cache_lengths
    )
    shallow_out = expert_layer(shallow_in, shallow_expert, shallow_gate, shallow_up, shallow_down)
    return expert_layer(shallow_out, deep_expert, deep_gate, deep_up, deep_down)


SLOTS = EXPERTS * CAP
PAD = 16
TALL = 56
META = 128
MIB = 1 << 20
STEP = 1024
FIRST_SHARE = 0.5625
F32 = jnp.float32
BF16 = jnp.bfloat16


def iota(shape, dim):
    return lax.broadcasted_iota(jnp.int32, shape, dim)


def to_column(row, count):
    same = iota((count, count), 0) == iota((count, count), 1)
    return jnp.sum(jnp.where(same, row, jnp.zeros_like(row)), axis=1, keepdims=True)


def to_row(column, count):
    same = iota((count, count), 0) == iota((count, count), 1)
    return jnp.sum(jnp.where(same, column, jnp.zeros_like(column)), axis=0, keepdims=True)


def ranks(id_row, id_column, count):
    earlier = iota((count, count), 1) < iota((count, count), 0)
    same = (id_row == id_column) & earlier
    return jnp.sum(same.astype(jnp.int32), axis=1, keepdims=True)


def split3(value):
    high = value.astype(BF16).astype(F32)
    middle = (value - high).astype(BF16).astype(F32)
    low = (value - high - middle).astype(BF16).astype(F32)
    return high, middle, low


def core_here():
    return lax.axis_index("tp") & 1


def dot(left, right):
    return jnp.dot(left, right, preferred_element_type=F32)


def params(mib):
    return pltpu.CompilerParams(vmem_limit_bytes=mib * MIB)


def cost(flops, moved):
    return pl.CostEstimate(flops=flops, bytes_accessed=moved, transcendentals=0)


VM = pl.BlockSpec(memory_space=pltpu.VMEM)
HB = pl.BlockSpec(memory_space=pltpu.HBM)


def attend_kernel(
    resid_in, query_in, key_in, value_in, keys_in, values_in, length_in,
    shallow_in, sgate_in, deep_in, dgate_in, up_in, out0, out1, out2, out3, home_ref,
    piece_ref,
    resid_ref, query_ref, key_ref, value_ref, keys_ref, values_ref, length_ref,
    shallow_ref, sgate_ref, deep_ref, dgate_ref, sems,
):
    rows, features = resid_ref.shape
    depth = keys_ref.shape[1]
    flat = rows * depth
    factor = 1.0 / math.sqrt(HD)
    order = (
        (query_in, query_ref), (keys_in, keys_ref), (key_in, key_ref), (length_in, length_ref),
        (values_in, values_ref), (value_in, value_ref), (resid_in, resid_ref),
        (shallow_in, shallow_ref), (sgate_in, sgate_ref), (deep_in, deep_ref), (dgate_in, dgate_ref),
    )
    copies = [pltpu.make_async_copy(a, b, sems.at[i]) for i, (a, b) in enumerate(order)]
    for copy in copies:
        copy.start()
    width = piece_ref.shape[1]
    others = pl.ds(pl.multiple_of((1 - core_here()) * (up_in.shape[1] // 2), 128), width)
    ahead = pltpu.make_async_copy(up_in.at[:, others], piece_ref, sems.at[len(order)])
    ahead.start()
    spread = (iota((features, META), 0) // HD == iota((features, META), 1)).astype(BF16)
    gather = (iota((META, features), 1) // HD == iota((META, features), 0)).astype(BF16)

    def head_sums(products):
        high = products.astype(BF16)
        low = (products - high.astype(F32)).astype(BF16)
        return dot(high, spread) + dot(low, spread)

    for copy in copies[:4]:
        copy.wait()
    query = query_ref[...].astype(F32)
    own = head_sums(query * key_ref[...].astype(F32)) * factor
    products = query[:, None, :] * keys_ref[...].astype(F32)
    cached = head_sums(products.reshape(flat, features)) * factor
    repeated = iota((flat, rows), 0) // depth == iota((flat, rows), 1)
    length = jnp.sum(jnp.where(repeated, length_ref[...], 0), axis=1, keepdims=True)
    valid = (iota((flat, META), 0) % depth) < length
    masked = jnp.where(valid, cached, -1e30).reshape(rows, depth, META)
    highest = jnp.maximum(jnp.max(masked, axis=1), own)
    past = jnp.exp(masked - highest[:, None, :])
    past = jnp.where(valid, past.reshape(flat, META), 0.0).reshape(rows, depth, META)
    own_exp = jnp.exp(own - highest)
    total = jnp.sum(past, axis=1) + own_exp
    weights = (past / total[:, None, :]).reshape(flat, META).astype(BF16)
    own_weight = (own_exp / total).astype(BF16)
    for copy in copies[4:]:
        copy.wait()
    wide = dot(weights, gather).reshape(rows, depth, features)
    attended = jnp.sum(wide * values_ref[...].astype(F32), axis=1)
    attended = attended + dot(own_weight, gather) * value_ref[...].astype(F32)
    states = (resid_ref[...].astype(F32) + attended).astype(BF16)

    here = lax.axis_index("ep")
    shallow = shallow_ref[...]
    deep = deep_ref[...]
    shallow_column = to_column(shallow, rows)
    deep_column = to_column(deep, rows)
    shallow_rank = ranks(shallow, shallow_column, rows)
    deep_rank = ranks(deep, deep_column, rows)
    place = (shallow_column ^ here) * PAD + shallow_rank
    home_ref[...] = jnp.broadcast_to((deep_column ^ here) * PAD + deep_rank, (rows, META))
    choose = (iota((EXPERTS * PAD, rows), 0) == to_row(place, rows)).astype(BF16)
    sent = dot(choose, states)
    lane = iota((rows, META), 1)
    shallow_gates = split3(to_column(sgate_ref[...], rows))
    deep_gates = split3(to_column(dgate_ref[...], rows))
    row = iota((PAD, META), 0)
    for at, out in enumerate((out0, out1, out2, out3)):
        to_shallow = (shallow_column == here ^ at) & (lane == shallow_rank)
        to_deep = (deep_column == here ^ at) & (lane == deep_rank)
        line = lambda kept, value: jnp.sum(jnp.where(kept, value, 0.0), axis=0, keepdims=True)
        apart = shallow_column ^ deep_column
        source = (apart * SLOTS + (shallow_column ^ here) * CAP + shallow_rank + 1).astype(F32)
        block = sent[at * PAD : (at + 1) * PAD]
        pieces = []
        for part in range(3):
            note = jnp.where(row == CAP, line(to_shallow, shallow_gates[part]), block[:, part * META : (part + 1) * META])
            note = jnp.where(row == CAP + 1, line(to_deep, deep_gates[part]), note)
            if part == 0:
                note = jnp.where(row == CAP + 2, line(to_deep, source), note)
            pieces.append(note)
        block = jnp.concatenate(pieces + [block[:, 3 * META :]], axis=1)
        out[...] = block.astype(BF16)
    ahead.wait()


def attend(arrays, up, width):
    rows, features = arrays[0].shape
    shape = jax.ShapeDtypeStruct((PAD, features), BF16)
    return pl.pallas_call(
        attend_kernel,
        in_specs=[HB] * (len(arrays) + 1),
        out_specs=[VM] * 6,
        out_shape=[shape] * 4 + [
            jax.ShapeDtypeStruct((rows, META), jnp.int32),
            jax.ShapeDtypeStruct((up.shape[0], width), BF16),
        ],
        scratch_shapes=[pltpu.VMEM(a.shape, a.dtype) for a in arrays]
        + [pltpu.SemaphoreType.DMA((len(arrays) + 1,))],
        compiler_params=params(16),
        name="attend",
    )(*[pltpu.with_memory_space_constraint(a, pltpu.HBM) for a in (*arrays, up)])


def load_kernel(weight_ref, after_ref, out_ref, sems):
    count = sems.shape[0]
    rows = weight_ref.shape[0] // count
    copies = [
        pltpu.make_async_copy(
            weight_ref.at[pl.ds(i * rows, rows)], out_ref.at[pl.ds(i * rows, rows)], sems.at[i]
        )
        for i in range(count)
    ]
    for copy in copies:
        copy.start()
    for copy in copies:
        copy.wait()


def load(weights, after):
    return pl.pallas_call(
        load_kernel,
        in_specs=[HB, pl.BlockSpec(memory_space=pl.ANY)],
        out_specs=VM,
        out_shape=jax.ShapeDtypeStruct(weights.shape, weights.dtype),
        scratch_shapes=[pltpu.SemaphoreType.DMA((4,))],
        compiler_params=params(4),
        cost_estimate=cost(0, 2 * weights.size),
        name="load",
    )(pltpu.with_memory_space_constraint(weights, pltpu.HBM), after)


def load_rest_kernel(first, weight_ref, after_ref, others_ref, own_ref, sems):
    half = own_ref.shape[1]
    rows = own_ref.shape[0] // 2
    ours = core_here() * half
    copies = []
    for base, ref in ((half - ours + first, others_ref), (ours, own_ref)):
        columns = pl.ds(pl.multiple_of(base, 128), ref.shape[1])
        for at in (0, rows):
            copies.append(
                pltpu.make_async_copy(
                    weight_ref.at[pl.ds(at, rows), columns],
                    ref.at[pl.ds(at, rows)],
                    sems.at[len(copies)],
                )
            )
    for copy in copies:
        copy.start()
    for copy in copies:
        copy.wait()


def load_rest(weights, after, first):
    rows, half = weights.shape[0], weights.shape[1] // 2
    return pl.pallas_call(
        functools.partial(load_rest_kernel, first),
        in_specs=[HB, pl.BlockSpec(memory_space=pl.ANY)],
        out_specs=[VM] * 2,
        out_shape=[
            jax.ShapeDtypeStruct((rows, half - first), weights.dtype),
            jax.ShapeDtypeStruct((rows, half), weights.dtype),
        ],
        scratch_shapes=[pltpu.SemaphoreType.DMA((4,))],
        compiler_params=params(4),
        cost_estimate=cost(0, 2 * weights.size),
        name="load_rest",
    )(pltpu.with_memory_space_constraint(weights, pltpu.HBM), after)


def choose_shallow():
    source = iota((TALL, EXPERTS * PAD), 1)
    kept = jnp.where(source % PAD < CAP, source // PAD * CAP + source % PAD, -1)
    return (kept == iota((TALL, EXPERTS * PAD), 0)).astype(BF16)


def notes_of(held):
    slot, lane = iota((TALL, META), 0), iota((TALL, META), 1)
    columns = []
    for row in range(CAP, CAP + 3):
        column = jnp.zeros((TALL, 1), F32)
        for at in range(EXPERTS):
            line = held[at * PAD + row : at * PAD + row + 1]
            value = line[:, :META]
            if row < CAP + 2:
                value = value + line[:, META : 2 * META] + line[:, 2 * META : 3 * META]
            kept = (slot - at * CAP == lane) & (lane < CAP)
            column = column + jnp.sum(jnp.where(kept, value, 0.0), axis=1, keepdims=True)
        columns.append(column)
    notes = jnp.where(lane == 0, columns[0], 0.0)
    notes = jnp.where(lane == 1, columns[1], notes)
    return jnp.where(lane == 2, columns[2], notes)


def up_block(rows, means, weights):
    product = dot(rows, weights)
    columns = product[SLOTS : SLOTS + 1]
    row = iota(product.shape, 0)
    centred = product - means * columns
    return row, centred, columns


def cuts_of(half):
    unit = 2 * META
    first = max(unit, int(half * FIRST_SHARE) // unit * unit)
    return (0, first), (first, half - first)


def columns_at(weight_ref, own, at, low, step):
    if low is not None:
        return weight_ref[:, at - low : at - low + step]
    half = weight_ref.shape[1] // 2
    which = core_here() if own else 1 - core_here()
    return weight_ref[:, pl.ds(pl.multiple_of(which * half + at, 128), step)]


def steps_of(width):
    return [(at, min(STEP, width - at)) for at in range(0, width, STEP)]


def send_block(rows_ref, means, weight_ref, start, low, sent_ref):
    for at, step in steps_of(sent_ref.shape[1]):
        weights = columns_at(weight_ref, False, start + at, low, step)
        row, centred, columns = up_block(rows_ref[...], means, weights)
        high = columns.astype(BF16).astype(F32)
        tail = jnp.where(row == SLOTS, high, jnp.where(row == SLOTS + 1, columns - high, 0.0))
        sent_ref[:, at : at + step] = jnp.where(row < SLOTS, centred, tail).astype(BF16)


def up_first_kernel(deep, start, low, *refs):
    if deep:
        notes_ref, h0, h1, h3, h2, weight_ref, rows_ref, stats_ref, sent_ref = refs
    else:
        h0, h1, h2, h3, weight_ref, rows_ref, stats_ref, sent_ref, notes_ref = refs
    held = jnp.concatenate([h0[...], h1[...], h2[...], h3[...]], axis=0)
    if deep:
        place = notes_ref[:, 2:3].astype(jnp.int32) - 1
        choose = (iota((TALL, held.shape[0]), 1) == place).astype(BF16)
    else:
        choose = choose_shallow()
        notes_ref[...] = notes_of(held.astype(F32))
    wide = dot(choose, held)
    rows_ref[...] = jnp.where(iota(wide.shape, 0) == SLOTS, 1.0, wide).astype(BF16)
    features = wide.shape[1]
    lane = iota((TALL, META), 1)
    total = jnp.sum(wide, axis=1, keepdims=True)
    square = jnp.sum(wide * wide, axis=1, keepdims=True)
    stats_ref[...] = jnp.where(lane == 0, total, jnp.where(lane == 1, square, 0.0))
    send_block(rows_ref, total / features, weight_ref, start, low, sent_ref)


def up_first(deep, cut, low, notes, held, weights):
    features = weights.shape[0]
    start, width = cut
    turn = (0, 1, 3, 2) if deep else (0, 1, 2, 3)
    operands = ([notes] if deep else []) + [held[k] for k in turn]
    note = jax.ShapeDtypeStruct((TALL, META), F32)
    out = pl.pallas_call(
        functools.partial(up_first_kernel, deep, start, low),
        in_specs=[VM] * (len(operands) + 1),
        out_specs=[VM] * (3 if deep else 4),
        out_shape=[
            jax.ShapeDtypeStruct((TALL, features), BF16),
            note,
            jax.ShapeDtypeStruct((TALL, width), BF16),
        ]
        + ([] if deep else [note]),
        compiler_params=params(8),
        cost_estimate=cost(2 * TALL * features * width, 2 * features * width),
        name="up_first",
    )(*operands, weights)
    return out if not deep else [*out, notes]


def up_other_kernel(start, low, rows_ref, stats_ref, weight_ref, *sent):
    for sent_ref in sent:
        send_block(rows_ref, stats_ref[:, 0:1] / rows_ref.shape[1], weight_ref, start, low, sent_ref)
        start += sent_ref.shape[1]


def up_other(rows, stats, weights, cut, low):
    start, width = cut
    features = weights.shape[0]
    return pl.pallas_call(
        functools.partial(up_other_kernel, start, low),
        in_specs=[VM] * 3,
        out_specs=[VM] * 2,
        out_shape=[jax.ShapeDtypeStruct((TALL, width // 2), BF16)] * 2,
        compiler_params=params(8),
        cost_estimate=cost(2 * TALL * features * width, 2 * features * width),
        name="up_other",
    )(rows, stats, weights)


def up_second_kernel(start, low, rows_ref, stats_ref, weight_ref, kept_ref):
    features = weight_ref.shape[0]
    means = stats_ref[:, 0:1] / features
    for at, step in steps_of(kept_ref.shape[1]):
        weights = columns_at(weight_ref, True, start + at, low, step)
        row, centred, columns = up_block(rows_ref[...], means, weights)
        kept_ref[:, at : at + step] = jnp.where(
            row < SLOTS, centred, jnp.where(row == SLOTS, columns, 0.0)
        )


def up_second(rows, stats, weights, cut, low):
    start, width = cut
    features = weights.shape[0]
    return pl.pallas_call(
        functools.partial(up_second_kernel, start, low),
        in_specs=[VM] * 3,
        out_specs=VM,
        out_shape=jax.ShapeDtypeStruct((TALL, width), F32),
        compiler_params=params(8),
        cost_estimate=cost(2 * TALL * features * width, 2 * features * width),
        name="up_second",
    )(rows, stats, weights)


def merge_into(features, source, width, got_refs, stats, other, sum_ref, sent_ref):
    apart = (stats[:, 0:1] - other[:, 0:1]) * (0.5 / features)
    held = jnp.zeros((SLOTS, META), F32)
    slot = iota((SLOTS, META), 0)
    span = width // len(got_refs)
    pieces = [(ref, i * span, at, step) for i, ref in enumerate(got_refs) for at, step in steps_of(span)]
    for got_ref, base, start, step in pieces:
        at = base + start
        kept = source(at, step)
        got = got_ref[:, start : start + step].astype(F32)
        mine = kept[SLOTS : SLOTS + 1]
        theirs = got[SLOTS : SLOTS + 1] + got[SLOTS + 1 : SLOTS + 2]
        row = iota(kept.shape, 0)
        columns = mine + theirs
        merged = jnp.where(row < SLOTS, kept + got + apart * (mine - theirs), columns)
        sum_ref[:, at : at + step] = merged
        sent_ref[:, at : at + step] = merged[:SLOTS].astype(BF16)
        for part in range(0, step, META):
            held = jnp.where(slot == (at + part) // META, columns[:, part : part + META], held)
    sent_ref[:, width : width + META] = held.astype(BF16)


def merge_kernel(features, kept_ref, got_ref, stats_ref, got_stats_ref, sent_ref, sum_ref, sums_ref):
    width = kept_ref.shape[1]
    stats, other = stats_ref[...], got_stats_ref[...]
    sums = stats + other
    sums_ref[...] = sums
    source = lambda at, step: kept_ref[:, at : at + step]
    merge_into(features, source, width, [got_ref], stats, other, sum_ref, sent_ref)
    lane = iota((SLOTS, META), 1)
    packed = jnp.zeros((SLOTS, META), F32)
    for which in range(2):
        for at, piece in enumerate(split3(sums[:SLOTS, which : which + 1])):
            packed = jnp.where(lane == 3 * which + at, piece, packed)
    sent_ref[:, width + META :] = packed.astype(BF16)


def merge(features, kept, got, stats, got_stats):
    width = kept.shape[1]
    return pl.pallas_call(
        functools.partial(merge_kernel, features),
        in_specs=[VM] * 4,
        out_specs=[VM] * 3,
        out_shape=[
            jax.ShapeDtypeStruct((SLOTS, width + 2 * META), BF16),
            jax.ShapeDtypeStruct((TALL, width), F32),
            jax.ShapeDtypeStruct((TALL, META), F32),
        ],
        compiler_params=params(8),
        name="merge",
    )(kept, got, stats, got_stats)


def up_merge_kernel(
    start, low, rows_ref, stats_ref, got_stats_ref, weight_ref, got0, got1, sent_ref, sum_ref
):
    features = weight_ref.shape[0]
    stats = stats_ref[...]
    means = stats[:, 0:1] / features

    def source(at, step):
        weights = columns_at(weight_ref, True, start + at, low, step)
        row, centred, columns = up_block(rows_ref[...], means, weights)
        return jnp.where(row < SLOTS, centred, jnp.where(row == SLOTS, columns, 0.0))

    got = [got0, got1]
    merge_into(features, source, sum_ref.shape[1], got, stats, got_stats_ref[...], sum_ref, sent_ref)


def up_merge(rows, stats, got_stats, weights, got, cut, low):
    start, width = cut
    features = weights.shape[0]
    return pl.pallas_call(
        functools.partial(up_merge_kernel, start, low),
        in_specs=[VM] * 6,
        out_specs=[VM] * 2,
        out_shape=[
            jax.ShapeDtypeStruct((SLOTS, width + META), BF16),
            jax.ShapeDtypeStruct((TALL, width), F32),
        ],
        compiler_params=params(8),
        cost_estimate=cost(2 * TALL * features * width, 2 * features * width),
        name="up_merge",
    )(rows, stats, got_stats, weights, *got)


def hidden_kernel(features, sum_ref, sums_ref, got_ref, packed_ref, *hidden):
    width = sum_ref.shape[1]
    packed = packed_ref[:, packed_ref.shape[1] - META :].astype(F32)
    held = got_ref[:, width : width + META].astype(F32)
    theirs_total = packed[:, 0:1] + packed[:, 1:2] + packed[:, 2:3]
    theirs_square = packed[:, 3:4] + packed[:, 4:5] + packed[:, 5:6]
    total, square = sums_ref[:SLOTS, 0:1], sums_ref[:SLOTS, 1:2]
    apart = (total - theirs_total) * (0.5 / (2 * features))
    center = (total + theirs_total) / D
    spread = (square + theirs_square) / D - center * center
    scale = lax.rsqrt(spread + epsilon)
    span = width // len(hidden)
    pieces = [(ref, i * span, at, step) for i, ref in enumerate(hidden) for at, step in steps_of(span)]
    for hidden_ref, base, start, step in pieces:
        at = base + start
        mine = sum_ref[:, at : at + step]
        got = got_ref[:, at : at + step].astype(F32)
        first = at // META
        theirs = jnp.concatenate([held[i : i + 1] for i in range(first, first + step // META)], axis=1)
        columns = mine[SLOTS : SLOTS + 1] - theirs
        pre = (mine[:SLOTS] + got + apart * columns) * scale
        hidden_ref[:, start : start + step] = jax.nn.gelu(pre, approximate=True).astype(BF16)


def hidden_units(features, total, sums, got, packed, count):
    return pl.pallas_call(
        functools.partial(hidden_kernel, features),
        in_specs=[VM] * 4,
        out_specs=[VM] * count,
        out_shape=[jax.ShapeDtypeStruct((SLOTS, total.shape[1] // count), BF16)] * count,
        compiler_params=params(8),
        cost_estimate=cost(1, 1),
        name="hidden",
    )(total, sums, got, packed)


def rows_at(weight_ref, own, start, width):
    half = weight_ref.shape[0] // 2
    which = core_here() if own else 1 - core_here()
    return weight_ref[pl.ds(pl.multiple_of(which * half + start, 128), width), :]


def down_part_kernel(own, start, count, weight_ref, *refs):
    hidden, earlier, out_ref = refs[:count], refs[count:-1], refs[-1]
    product = None
    for part in hidden:
        width = part.shape[1]
        term = dot(part[...], rows_at(weight_ref, own, start, width))
        product = term if product is None else product + term
        start += width
    for part in earlier:
        product = product + part[...]
    out_ref[...] = product


def down_part(hidden, weights, own, cut, *earlier):
    features = weights.shape[1]
    return pl.pallas_call(
        functools.partial(down_part_kernel, own, cut[0], len(hidden)),
        in_specs=[VM] * (1 + len(hidden) + len(earlier)),
        out_specs=VM,
        out_shape=jax.ShapeDtypeStruct((SLOTS, features), F32),
        compiler_params=params(8),
        cost_estimate=cost(1, 1),
        name="down_part",
    )(weights, *hidden, *earlier)


def down_last_kernel(deep, start, part_ref, rows_ref, notes_ref, hidden_ref, weight_ref, *outs):
    features = weight_ref.shape[1]
    weights = rows_at(weight_ref, False, start, hidden_ref.shape[1])
    total = part_ref[...] + dot(hidden_ref[...], weights)
    which = 1 if deep else 0
    gate = notes_ref[:SLOTS, which : which + 1]
    result = rows_ref[...].astype(F32)[:SLOTS] + gate * total
    if not deep:
        outs[0][...] = result.astype(BF16)
    else:
        target = iota((EXPERTS * PAD, SLOTS), 0)
        kept = jnp.where(target % PAD < CAP, target // PAD * CAP + target % PAD, -1)
        spread = (kept == iota((EXPERTS * PAD, SLOTS), 1)).astype(BF16)
        placed = dot(spread, result.astype(BF16))
        for at, out in enumerate(outs):
            out[...] = placed[at * PAD : (at + 1) * PAD].astype(BF16)


def down_last(deep, part, rows, notes, hidden, weights, cut):
    start, width = cut
    features = weights.shape[1]
    shapes = [(PAD, features)] * EXPERTS if deep else [(SLOTS, features)]
    return pl.pallas_call(
        functools.partial(down_last_kernel, deep, start),
        in_specs=[VM] * 5,
        out_specs=[VM] * len(shapes),
        out_shape=[jax.ShapeDtypeStruct(shape, BF16) for shape in shapes],
        compiler_params=params(8),
        cost_estimate=cost(2 * SLOTS * features * width, 2 * features * width),
        name="down_last",
    )(part, rows, notes, hidden, weights)


def finish_kernel(home_ref, g0, g1, g2, g3, out_ref):
    rows = out_ref.shape[0]
    choose = (iota((rows, EXPERTS * PAD), 1) == home_ref[:, 0:1]).astype(BF16)
    held = jnp.concatenate([g0[...], g1[...], g2[...], g3[...]], axis=0)
    out_ref[...] = dot(choose, held).astype(BF16)


def finish(home, got):
    return pl.pallas_call(
        finish_kernel,
        in_specs=[VM] * 5,
        out_specs=VM,
        out_shape=jax.ShapeDtypeStruct((home.shape[0], got[0].shape[1]), BF16),
        compiler_params=params(8),
        name="finish",
    )(home, *got)


def swap(value, axis, apart):
    count = lax.axis_size(axis)
    return lax.ppermute(value, axis, [(i, i ^ apart) for i in range(count)])


def swap_all(blocks, order=(1, 2, 3)):
    got = {k: swap(blocks[k], "ep", k) for k in order}
    return [blocks[0]] + [got[k] for k in (1, 2, 3)]


def after(value, earlier):
    return lax.optimization_barrier((value, earlier))[0]


def expert_block(deep, notes, held, up, down):
    up_first_piece, up_other_piece, up_own = up
    features = up_own.shape[0]
    first, second = cuts_of(down.shape[0] // 2)
    low = (None, None) if deep else (0, second[0])
    rows, stats, sent_a, notes = up_first(deep, first, low[0], notes, held, up_first_piece)
    got_a, got_stats = swap(sent_a, "tp", 1), swap(stats, "tp", 1)
    kept = up_second(rows, stats, up_own, first, low[0])
    sent_a, total_a, sums = merge(features, kept, got_a, stats, got_stats)
    over_a = swap(sent_a, "tp", 2)
    later = after(rows, sent_a)
    got_b = [swap(sent, "tp", 1) for sent in up_other(later, stats, up_other_piece, second, low[1])]
    sent_b, total_b = up_merge(later, stats, got_stats, up_own, got_b, second, low[0])
    over_b = swap(sent_b, "tp", 2)
    hidden_a = hidden_units(features, after(total_a, sent_b), sums, over_a, over_a, 2)
    other_a = [swap(hidden, "tp", 1) for hidden in hidden_a]
    part = down_part(hidden_a, down, True, first)
    part = down_part(other_a, down, False, first, part)
    (hidden_b,) = hidden_units(features, after(total_b, part), sums, over_b, over_a, 1)
    other_b = swap(hidden_b, "tp", 1)
    part = down_part([hidden_b], down, True, second, part)
    return notes, down_last(deep, part, rows, notes, other_b, down, second)


def fast_body(
    resid,
    query,
    new_key,
    new_value,
    cache_keys,
    cache_values,
    cache_lengths,
    shallow_expert,
    shallow_gate,
    shallow_up,
    shallow_down,
    deep_expert,
    deep_gate,
    deep_up,
    deep_down,
):
    rows = resid.shape[0]
    width = cuts_of(shallow_down.shape[0] // 2)[0][1]
    *blocks, home, piece = attend(
        (
            resid,
            query,
            new_key,
            new_value,
            cache_keys,
            cache_values,
            cache_lengths.reshape(1, rows),
            shallow_expert.reshape(1, rows),
            shallow_gate.reshape(1, rows),
            deep_expert.reshape(1, rows),
            deep_gate.reshape(1, rows),
        ),
        shallow_up,
        width,
    )
    others, own = load_rest(shallow_up, blocks[0], width)
    piece = after(piece, own)
    weights = (piece, others, own)
    notes, (between,) = expert_block(False, None, swap_all(blocks), weights, shallow_down)
    weights = (load(deep_up, between),) * 3
    held = swap_all([between] * EXPERTS, (1, 3, 2))
    _, blocks = expert_block(True, notes, held, weights, deep_down)
    return finish(home, swap_all(blocks))


def solution(mesh):
    fits = mesh.shape["ep"] == EXPERTS and mesh.shape["tp"] == 4
    return jax.shard_map(
        fast_body if fits else general_body,
        mesh=mesh,
        in_specs=(
            P(("groups", "ep"), "tp"),
            P(("groups", "ep"), "tp"),
            P(("groups", "ep"), "tp"),
            P(("groups", "ep"), "tp"),
            P(("groups", "ep"), None, "tp"),
            P(("groups", "ep"), None, "tp"),
            P(("groups", "ep")),
            P(("groups", "ep"), None),
            P(("groups", "ep")),
            P("tp", "ep"),
            P("ep", "tp"),
            P(("groups", "ep"), None),
            P(("groups", "ep")),
            P("tp", "ep"),
            P("ep", "tp"),
        ),
        out_specs=P(("groups", "ep"), "tp"),
        check_vma=False,
    )
```
